256 devices in a mesh: tok: 64 (over y, x, z_hi, core), hid: 4 (over z_lo).
Axes of the slice: x: 4, y: 4, z: 8 (z_hi: 2, z_lo: 4; z = z_hi * 4 + z_lo), core: 2. Of those that a mesh axis runs over, the one named last changes fastest.
Arguments:
- block_input: bfloat16 [512, 128, 1024], P('hid', 'tok'), may hold values from -6 to 6
- out_grad: bfloat16 [512, 128, 1024], P('hid', 'tok'), may hold values from -6 to 6
- norm_gain: float32 [128, 1024], P('tok'), may hold values from 0.25 to 1.75
- w_in: bfloat16 [128, 1024, 2048], P('tok', None, 'hid'), may hold values from -0.1875 to 0.1875
- w_out: bfloat16 [128, 2048, 1024], P('tok', 'hid'), may hold values from -0.125 to 0.125
Outputs:
- input_grad: bfloat16 [512, 128, 1024], P('hid', 'tok')
- grad_in: bfloat16 [128, 1024, 2048], P('tok', None, 'hid')
- grad_out: bfloat16 [128, 2048, 1024], P('tok', 'hid')
The draws below stay inside these ranges and needn't reach their ends.
All inputs are finite; a program needn't handle non-finite values.
Results may differ from the reference program's by a relative error of at most 0.0061.
Values may be sent and summed in bfloat16 or wider, within the bound.
A program may use at most 64 MiB of HBM per device.

```python
import jax
import jax.numpy as jnp
from jax import lax

TOKENS = 128
WIDTH = 1024
HIDDEN_SIZE = 2048
SAMPLES = 512


def level_of(rng, extent, pieces, least, largest):
    level, own = 1.0, jax.random.fold_in(rng, 6)
    for axis_at, shards_of in pieces:
        heights = jnp.exp(jax.random.uniform(jax.random.fold_in(own, axis_at), (shards_of,), jnp.float32, least / len(pieces), largest / len(pieces)))
        level = level * jnp.repeat(heights, extent[axis_at] // shards_of).reshape([-1 if axis == axis_at else 1 for axis in range(len(extent))])
    return level


def scatter_about(own_key, extent, scale, reach, split=(), kind=jnp.bfloat16):
    result = scale * jax.random.normal(own_key, extent, jnp.float32)
    if split:
        result = result * level_of(own_key, extent, split, -0.22, 0.18)
    return jnp.clip(result, -reach, reach).astype(kind)


def setup_inputs(seed: int = 0) -> dict:
    streams_of = jax.random.split(jax.random.key(seed), 6)
    return {
        "block_input": scatter_about(streams_of[0], (SAMPLES, TOKENS, WIDTH), 1.0, 6.0, ((0, 4), (1, 64))),
        "out_grad": scatter_about(streams_of[1], (SAMPLES, TOKENS, WIDTH), 1.0, 6.0, ((0, 4), (1, 64))),
        "norm_gain": jnp.clip(1.0 + 0.15 * jax.random.normal(streams_of[2], (TOKENS, WIDTH), jnp.float32), 0.25, 1.75),
        "w_in": scatter_about(streams_of[3], (TOKENS, WIDTH, HIDDEN_SIZE), WIDTH ** -0.5, 0.1875, ((0, 64), (2, 4))),
        "w_out": scatter_about(streams_of[4], (TOKENS, HIDDEN_SIZE, WIDTH), HIDDEN_SIZE ** -0.5, 0.125, ((0, 64), (1, 4))),
    }


EPS = 1e-06

def gelu_tanh(value):
    return 0.5 * value * (1.0 + jnp.tanh(0.7978845608 * (value + 0.044715 * value * value * value)))

def swap_heads(array):
    samples, count, width = array.shape
    return array.reshape(samples, count, count, width // count).transpose(0, 2, 1, 3).reshape(samples, count, width)

def per_token(operands):
    mixed_row, grad_row, gain_row, first, second = operands
    mixed_f = mixed_row.astype(jnp.float32)
    scale = lax.rsqrt(lax.optimization_barrier(jnp.mean(mixed_f * mixed_f, axis=-1, keepdims=True)) + EPS)
    normed = (mixed_f * scale * gain_row).astype(jnp.bfloat16)
    pre = jnp.dot(normed, first, preferred_element_type=jnp.float32)
    act, pull = jax.vjp(gelu_tanh, pre)
    act_b = act.astype(jnp.bfloat16)
    act_grad = jnp.dot(grad_row, second.T, preferred_element_type=jnp.float32)
    pre_grad = pull(act_grad)[0].astype(jnp.bfloat16)
    grad_second = jnp.dot(act_b.T, grad_row, preferred_element_type=jnp.float32).astype(jnp.bfloat16)
    grad_first = jnp.dot(normed.T, pre_grad, preferred_element_type=jnp.float32).astype(jnp.bfloat16)
    normed_grad = jnp.dot(pre_grad, first.T, preferred_element_type=jnp.float32)
    upper = normed_grad * gain_row
    inner = lax.optimization_barrier(jnp.sum(upper * mixed_f, axis=-1, keepdims=True))
    mixed_grad_in = (scale * upper - mixed_f * scale * scale * scale * inner / WIDTH).astype(jnp.bfloat16)
    return (mixed_grad_in, grad_first, grad_second)

def reference(block_input, out_grad, norm_gain, w_in, w_out):
    mixed = swap_heads(block_input).transpose(1, 0, 2)
    mixed_grad = swap_heads(out_grad).transpose(1, 0, 2)
    mixed_in, grad_in, grad_out = lax.map(per_token, (mixed, mixed_grad, norm_gain, w_in, w_out))
    back = swap_heads(mixed_in.transpose(1, 0, 2))
    input_grad = (out_grad.astype(jnp.float32) + back.astype(jnp.float32)).astype(jnp.bfloat16)
    return (input_grad, grad_in, grad_out)
```

```python
import functools

import jax
import jax.numpy as jnp
from jax import lax
from jax.experimental import pallas as pl
from jax.experimental.pallas import tpu as pltpu
from jax.sharding import PartitionSpec as P

TOKENS = 128
WIDTH = 1024
HEAD = 8
EPS = 1e-06
MESH = pl.DeviceIdType.MESH

COLUMNS = 16
PEERS = 32
PLANES = 8
OUT, PASS = 8, 9

LEFT = {
    0: [(OUT, "c0x"), (PASS, "c1x")],
    1: [(OUT, PASS), ("s1", "s1"), ("s2", "s2"), ("s3", "s3"), ("c0", "c0"), ("c1", "c1")],
    2: [("s2", "s2"), ("s3", "s3"), ("c0", "c0"), ("c1", "c1")],
    3: [("s3", "s3"), ("c0", "c0"), ("c1", "c1")],
}


def mirrored(slot):
    if not isinstance(slot, str):
        return slot
    return slot[0] + str(3 - int(slot[1])) + slot[2:]


RIGHT = {3 - zl: [(mirrored(a), mirrored(b)) for a, b in items] for zl, items in LEFT.items()}

BACK_RIGHT = {
    0: ["c1", "c0", "s3", "s2", "p1", "s1"],
    1: ["c1", "c0", "s3", "s2"],
    2: ["c1", "c0", "s3"],
    3: ["c1", "c0"],
}
BACK_LEFT = {3 - zl: [mirrored(a) for a in items] for zl, items in BACK_RIGHT.items()}


def place():
    tok, zl = lax.axis_index("tok"), lax.axis_index("hid")
    core, half, column = lax.rem(tok, 2), lax.rem(tok // 2, 2), tok // 4
    return column, half, core, zl


def device(column, half, core, zl):
    return (column * 4 + half * 2 + core, zl)


def z_neighbour(column, half, core, zl, step):
    z = lax.rem(half * 4 + zl + PLANES + step, PLANES)
    return device(column, z // 4, core, lax.rem(z, 4))


def plane_peer(column, half, core, zl, ahead):
    peer = lax.rem(column * 2 + core + ahead, PEERS)
    return peer, device(peer // 2, half, lax.rem(peer, 2), zl)


def wait_for(ref, sem):
    pltpu.make_async_copy(ref, ref, sem).wait()


def greet(here):
    barrier = pltpu.get_barrier_semaphore()

    def signal(ahead, carry):
        _, target = plane_peer(*here, ahead)
        pl.semaphore_signal(barrier, inc=1, device_id=target, device_id_type=MESH)
        return carry

    lax.fori_loop(1, PEERS, signal, 0)
    for step in (-1, 1):
        pl.semaphore_signal(barrier, inc=1, device_id=z_neighbour(*here, step), device_id_type=MESH)
    pl.semaphore_wait(barrier, PEERS + 1)


def slot_of(name, half):
    if not isinstance(name, str):
        return name
    k = int(name[1])
    if name.endswith("x") or name[0] == "s":
        return half * 4 + k
    return (1 - half) * 4 + k


def out_kernel(parts_ref, slots_out, slots, plane_send, plane_recv, ring_send, ring_recv, keep_sem):
    here = place()
    column, half, core, zl = here
    me = column * 2 + core
    own = half * 4 + zl
    greet(here)

    for which, (part, slot) in enumerate(((1 - half, OUT), (half, own))):

        def send(ahead, carry, which=which, part=part, slot=slot):
            peer, target = plane_peer(*here, ahead)
            pltpu.make_async_remote_copy(
                src_ref=parts_ref.at[part, peer],
                dst_ref=slots.at[slot, :, :, me],
                send_sem=plane_send.at[which],
                recv_sem=plane_recv.at[which],
                device_id=target,
                device_id_type=MESH,
            ).start()
            return carry

        lax.fori_loop(1, PEERS, send, 0)
        pltpu.make_async_copy(
            parts_ref.at[part, me], slots.at[slot, :, :, me], plane_recv.at[which]
        ).start()
    wait_for(slots.at[OUT], plane_recv.at[0])
    wait_for(slots.at[own], plane_recv.at[1])

    targets = (z_neighbour(*here, -1), z_neighbour(*here, 1))
    for case in range(4):

        @pl.when(zl == case)
        def _(case=case):
            lists = (LEFT[case], RIGHT[case])
            waited = {"s" + str(case)}
            sends = []
            names = ["s0", "s1", "s2", "s3", "c0", "c1", "c2", "c3"]
            if case in (0, 3):
                names.append(PASS)
            for turn in range(max(len(items) for items in lists)):
                for way in (0, 1):
                    if turn >= len(lists[way]):
                        continue
                    source, goal = lists[way][turn]
                    at = slot_of(source, half)
                    if source != OUT and source not in waited:
                        wait_for(slots.at[at], ring_recv.at[at])
                        waited.add(source)
                    to = slot_of(goal, half)
                    copy = pltpu.make_async_remote_copy(
                        src_ref=slots.at[at],
                        dst_ref=slots.at[to],
                        send_sem=ring_send.at[way, turn],
                        recv_sem=ring_recv.at[to],
                        device_id=targets[way],
                        device_id_type=MESH,
                    )
                    copy.start()
                    sends.append(copy)
            for name in names:
                if name not in waited:
                    at = slot_of(name, half)
                    wait_for(slots.at[at], ring_recv.at[at])
            for copy in sends:
                copy.wait_send()

    keep = pltpu.make_async_copy(slots.at[pl.ds(0, PLANES)], slots_out, keep_sem)
    keep.start()
    keep.wait()
    for which in (0, 1):
        wait_for(parts_ref.at[which, pl.ds(0, PEERS - 1)], plane_send.at[which])


def back_kernel(
    sums_ref, got_out, got, from_left, from_right, final, ring_send, left_recv, right_recv, plane_send, plane_recv, keep_sem
):
    here = place()
    column, half, core, zl = here
    me = column * 2 + core
    greet(here)
    targets = (z_neighbour(*here, -1), z_neighbour(*here, 1))

    def add(ref, at, plane):
        ref[at] = (ref[at].astype(jnp.float32) + sums_ref[plane].astype(jnp.float32)).astype(jnp.bfloat16)

    for case in range(4):

        @pl.when(zl == case)
        def _(case=case):
            lists = (BACK_LEFT[case], BACK_RIGHT[case])
            buffers = (from_right, from_left)
            arrived = (right_recv, left_recv)
            sends = []
            for turn in range(max(len(items) for items in lists)):
                for way in (0, 1):
                    if turn >= len(lists[way]):
                        continue
                    item = lists[way][turn]
                    into, recv = buffers[way], arrived[way]
                    starts = case == (3, 0)[way]
                    ends = case == (0, 3)[way]
                    if item[0] == "p":
                        at = half * 4 + int(item[1])
                        wait_for(into.at[at], recv.at[at])
                        source, to = into.at[at], PLANES
                    else:
                        at = slot_of(item, half)
                        to = at
                        if starts:
                            source = sums_ref.at[at]
                        else:
                            wait_for(into.at[at], recv.at[at])
                            add(into, at, at)
                            source = into.at[at]
                    copy = pltpu.make_async_remote_copy(
                        src_ref=source,
                        dst_ref=into.at[to],
                        send_sem=ring_send.at[way, turn],
                        recv_sem=recv.at[to],
                        device_id=targets[way],
                        device_id_type=MESH,
                    )
                    copy.start()
                    sends.append(copy)
            own = half * 4 + case
            total = sums_ref[own].astype(jnp.float32)
            if case > 0:
                wait_for(from_left.at[own], left_recv.at[own])
                total = total + from_left[own].astype(jnp.float32)
            if case < 3:
                wait_for(from_right.at[own], right_recv.at[own])
                total = total + from_right[own].astype(jnp.float32)
            final[half] = total.astype(jnp.bfloat16)
            into, recv = (from_left, left_recv) if case < 2 else (from_right, right_recv)
            at = PLANES if case in (1, 2) else own
            wait_for(into.at[at], recv.at[at])
            final[1 - half] = into[at]
            for copy in sends:
                copy.wait_send()

    def send(ahead, carry):
        peer, target = plane_peer(*here, ahead)
        pltpu.make_async_remote_copy(
            src_ref=final.at[:, :, peer],
            dst_ref=got.at[me],
            send_sem=plane_send,
            recv_sem=plane_recv,
            device_id=target,
            device_id_type=MESH,
        ).start()
        return carry

    lax.fori_loop(1, PEERS, send, 0)
    pltpu.make_async_copy(final.at[:, :, me], got.at[me], plane_recv).start()
    wait_for(got, plane_recv)
    keep = pltpu.make_async_copy(got, got_out, keep_sem)
    keep.start()
    keep.wait()
    wait_for(got.at[pl.ds(0, PEERS - 1)], plane_send)


def gelu_tanh(value):
    return 0.5 * value * (1.0 + jnp.tanh(0.7978845608 * (value + 0.044715 * value * value * value)))


def by_peer(array):
    samples, local_tok, width = array.shape
    split = array.reshape(samples, local_tok, COLUMNS, 2, 2, 2, HEAD)
    split = split.transpose(3, 2, 4, 5, 1, 6, 0)
    return split.reshape(2, PEERS, 2, local_tok * HEAD, samples)


def per_device(block_input, out_grad, norm_gain, w_in, w_out):
    own_rows, local_tok, width = block_input.shape
    gain_col = norm_gain[:, :, None]
    rows = local_tok * HEAD
    parts = jnp.stack([by_peer(block_input), by_peer(out_grad)], axis=2)
    block = (2, 2, PEERS, rows, own_rows)
    slots = pl.pallas_call(
        out_kernel,
        out_shape=jax.ShapeDtypeStruct((PLANES, *block), jnp.bfloat16),
        in_specs=[pl.BlockSpec(memory_space=pltpu.VMEM)],
        out_specs=pl.BlockSpec(memory_space=pl.ANY),
        scratch_shapes=[
            pltpu.VMEM((PLANES + 2, *block), jnp.bfloat16),
            pltpu.SemaphoreType.DMA((2,)),
            pltpu.SemaphoreType.DMA((2,)),
            pltpu.SemaphoreType.DMA((2, 6)),
            pltpu.SemaphoreType.DMA((PLANES + 2,)),
            pltpu.SemaphoreType.DMA,
        ],
        compiler_params=pltpu.CompilerParams(
            collective_id=0, has_side_effects=True, vmem_limit_bytes=40 * 2**20
        ),
    )(parts)
    slots = slots.reshape(2, 4, 2, 2, COLUMNS, 2 * rows, own_rows)
    slots = slots.transpose(2, 3, 4, 0, 5, 1, 6).reshape(2, 2, width, 4 * own_rows)
    mixed_all, dmix_all = slots[0], slots[1]
    mixed_f = mixed_all.astype(jnp.float32)
    scale = lax.rsqrt(jnp.mean(mixed_f * mixed_f, axis=1, keepdims=True) + EPS)
    normed_all = (mixed_f * scale * gain_col).astype(jnp.bfloat16)
    pre = jnp.einsum("tdb,tdf->tbf", normed_all, w_in, preferred_element_type=jnp.float32)
    act, pull = jax.vjp(gelu_tanh, pre)
    act_b = act.astype(jnp.bfloat16)
    act_grad = jnp.einsum("tdb,tfd->tbf", dmix_all, w_out, preferred_element_type=jnp.float32)
    pre_grad = pull(act_grad)[0].astype(jnp.bfloat16)
    partial_grad = jnp.einsum("tbf,tdf->tdb", pre_grad, w_in, preferred_element_type=jnp.float32)
    upper = partial_grad * gain_col
    inner = jnp.sum(upper * mixed_f, axis=1, keepdims=True)
    back = (scale * upper - mixed_f * scale * scale * scale * inner / WIDTH).astype(jnp.bfloat16)
    back = back.reshape(2, COLUMNS, 2, 2 * rows, 4, own_rows).transpose(2, 4, 0, 1, 3, 5)
    back = back.reshape(PLANES, 2, PEERS, rows, own_rows)
    got = pl.pallas_call(
        back_kernel,
        out_shape=jax.ShapeDtypeStruct((PEERS, 2, 2, rows, own_rows), jnp.bfloat16),
        in_specs=[pl.BlockSpec(memory_space=pltpu.VMEM)],
        out_specs=pl.BlockSpec(memory_space=pl.ANY),
        scratch_shapes=[
            pltpu.VMEM((PEERS, 2, 2, rows, own_rows), jnp.bfloat16),
            pltpu.VMEM((PLANES + 1, 2, PEERS, rows, own_rows), jnp.bfloat16),
            pltpu.VMEM((PLANES + 1, 2, PEERS, rows, own_rows), jnp.bfloat16),
            pltpu.VMEM((2, 2, PEERS, rows, own_rows), jnp.bfloat16),
            pltpu.SemaphoreType.DMA((2, 6)),
            pltpu.SemaphoreType.DMA((PLANES + 1,)),
            pltpu.SemaphoreType.DMA((PLANES + 1,)),
            pltpu.SemaphoreType.DMA,
            pltpu.SemaphoreType.DMA,
            pltpu.SemaphoreType.DMA,
        ],
        compiler_params=pltpu.CompilerParams(
            collective_id=1, has_side_effects=True, vmem_limit_bytes=40 * 2**20
        ),
    )(back)
    grad_out = jnp.einsum(
        "tbf,tdb->tfd", act_b, dmix_all, preferred_element_type=jnp.float32
    ).astype(jnp.bfloat16)
    grad_in = jnp.einsum(
        "tdb,tbf->tdf", normed_all, pre_grad, preferred_element_type=jnp.float32
    ).astype(jnp.bfloat16)
    got = got.reshape(COLUMNS, 2, 2, 2, local_tok, HEAD, own_rows).transpose(6, 4, 0, 2, 1, 3, 5)
    returned = got.reshape(own_rows, local_tok, width)
    input_grad = (out_grad.astype(jnp.float32) + returned.astype(jnp.float32)).astype(jnp.bfloat16)
    return (input_grad, grad_in, grad_out)


def solution(mesh):
    in_specs = (
        P("hid", "tok", None),
        P("hid", "tok", None),
        P("tok", None),
        P("tok", None, "hid"),
        P("tok", "hid", None),
    )
    out_specs = (P("hid", "tok", None), P("tok", None, "hid"), P("tok", "hid", None))
    return jax.shard_map(
        per_device, mesh=mesh, in_specs=in_specs, out_specs=out_specs, check_vma=False
    )
```

```python
import jax
import jax.numpy as jnp
from jax import lax
from jax.experimental import pallas as pl
from jax.experimental.pallas import tpu as pltpu
from jax.sharding import PartitionSpec as P

WIDTH = 1024
HEAD = 8
EPS = 1e-06
MESH = pl.DeviceIdType.MESH

COLUMNS = 16
PEERS = 32
PLANES = 8
OUT, PASS = 8, 9
DEPTH = 2
TAIL = 4

ORDER = {
    0: [
        "f.l.o.c0.1", "f.r.s0.s0.0", "f.l.p.c1.0", "f.r.c3.c3.1", "f.l.p.c1.1", "f.r.c2.c2.0", "f.r.c2.c2.1", "f.l.o.c0.0", "f.r.s0.s0.1", "m.2.1",
        "b.r.s2.1", "m.3.0", "b.r.s3.0", "f.r.c3.c3.0", "m.0.1", "b.r.c0.1", "m.1.0", "b.r.c1.0", "b.r.s1.0", "m.1.1",
        "b.r.s1.1", "b.r.c1.1", "m.0.0", "b.r.c0.0", "m.3.1", "b.r.s3.1", "m.2.0", "b.l.c2.0", "b.r.s2.0", "b.l.c2.1",
        "b.r.p1.0", "b.l.c3.1", "b.l.c3.0", "b.r.p1.1", "w.0", "e.1", "e.0", "w.1", "w.2", "w.3",
    ],
    1: [
        "f.l.o.p.0", "f.l.o.p.1", "f.r.s1.s1.0", "f.l.s1.s1.1", "f.r.s1.s1.1", "f.l.s1.s1.0", "f.r.s0.s0.0", "f.r.c3.c3.1", "f.l.s2.s2.1", "m.2.0",
        "f.l.s3.s3.0", "f.r.c2.c2.0", "f.l.c0.c0.1", "f.r.c2.c2.1", "m.1.0", "f.l.c1.c1.0", "f.r.s0.s0.1", "m.1.1", "f.l.c1.c1.1", "f.r.c3.c3.0",
        "f.l.s3.s3.1", "b.r.c1.0", "f.l.c0.c0.0", "m.3.0", "b.r.s3.0", "m.0.0", "f.l.s2.s2.0", "m.0.1", "b.r.c0.1", "b.r.c1.1",
        "b.l.c2.0", "m.2.1", "b.r.s2.1", "b.l.c2.1", "b.r.c0.0", "m.3.1", "b.l.c3.1", "w.0", "b.r.s3.1", "w.1",
        "b.l.c3.0", "b.r.s2.0", "b.l.s0.1", "w.2", "w.3", "b.l.s0.0", "e.0", "e.1",
    ],
    2: [
        "f.r.o.p.0", "f.r.o.p.1", "f.l.s2.s2.0", "f.r.s2.s2.1", "f.l.s2.s2.1", "f.r.s2.s2.0", "f.l.s3.s3.0", "f.l.c0.c0.1", "f.r.s1.s1.1", "m.1.0",
        "f.r.s0.s0.0", "f.l.c1.c1.0", "f.r.c3.c3.1", "f.l.c1.c1.1", "m.2.0", "f.r.c2.c2.0", "f.l.s3.s3.1", "m.2.1", "f.r.c2.c2.1", "f.l.c0.c0.0",
        "f.r.s0.s0.1", "b.l.c2.0", "f.r.c3.c3.0", "m.0.0", "b.l.s0.0", "m.3.0", "f.r.s1.s1.0", "m.3.1", "b.l.c3.1", "b.l.c2.1",
        "b.r.c1.0", "m.1.1", "b.l.s1.1", "b.r.c1.1", "b.l.c3.0", "m.0.1", "b.r.c0.1", "w.0", "b.l.s0.1", "w.1",
        "b.r.c0.0", "b.l.s1.0", "b.r.s3.1", "w.2", "w.3", "b.r.s3.0", "e.0", "e.1",
    ],
    3: [
        "f.r.o.c3.1", "f.l.s3.s3.0", "f.r.p.c2.0", "f.l.c0.c0.1", "f.r.p.c2.1", "f.l.c1.c1.0", "f.l.c1.c1.1", "f.r.o.c3.0", "f.l.s3.s3.1", "m.1.1",
        "b.l.s1.1", "m.0.0", "b.l.s0.0", "f.l.c0.c0.0", "m.3.1", "b.l.c3.1", "m.2.0", "b.l.c2.0", "b.l.s2.0", "m.2.1",
        "b.l.s2.1", "b.l.c2.1", "m.3.0", "b.l.c3.0", "m.0.1", "b.l.s0.1", "m.1.0", "b.r.c1.0", "b.l.s1.0", "b.r.c1.1",
        "b.l.p2.0", "b.r.c0.1", "b.r.c0.0", "b.l.p2.1", "w.0", "e.1", "e.0", "w.1", "w.2", "w.3",
    ],
}


def place():
    tok, zl = lax.axis_index("tok"), lax.axis_index("hid")
    core, half, column = lax.rem(tok, 2), lax.rem(tok // 2, 2), tok // 4
    return column, half, core, zl


def device(column, half, core, zl):
    return (column * 4 + half * 2 + core, zl)


def z_neighbour(column, half, core, zl, step):
    z = lax.rem(half * 4 + zl + PLANES + step, PLANES)
    return device(column, z // 4, core, lax.rem(z, 4))


def plane_peer(column, half, core, zl, ahead):
    peer = lax.rem(column * 2 + core + ahead, PEERS)
    return peer, device(peer // 2, half, lax.rem(peer, 2), zl)


def wait_for(ref, sem):
    pltpu.make_async_copy(ref, ref, sem).wait()


def dot(left, right, dims):
    return lax.dot_general(left, right, (dims, ((), ())), preferred_element_type=jnp.float32)


def steps_of(case):
    parts, mlps, now = [], [], []
    here = set()
    sent = {"l": [], "r": []}

    def arrive(name, head):
        if (name, head) not in here:
            here.add((name, head))
            kind = {"o": "out", f"s{case}": "own"}.get(name, "arrived")
            now.append((kind, name, int(head)))

    for item in ORDER[case]:
        item = item.split(".")
        if item[0] in "mw":
            if item[0] == "m":
                mlps.append((int(item[1]), int(item[2])))
                arrive("s" + item[1], item[2])
                arrive("c" + item[1], item[2])
            parts.append(now)
            now = []
            continue
        if item[0] == "e":
            now.append(("end", int(item[1])))
            continue
        if item[0] == "f":
            arrive(item[2], item[-1])
        turns = sent[item[1]]
        late = len(turns) - DEPTH
        if late >= 0:
            now.append(("sent", turns[late], item[1], late))
        now.append((item[0], *item[1:-1], int(item[-1]), len(turns)))
        turns.append(item[0])
        if len(sent["l"]) + len(sent["r"]) == 3:
            now.append(("prepare",))
    parts.append(now)
    for way, turns in sent.items():
        parts[-1] += [("sent", turns[late], way, late) for late in range(max(0, len(turns) - DEPTH), len(turns))]
    return parts, mlps


def kernel(
    input_ref, cotangent_ref, gain_ref, w_in_ref, w_out_ref, returned_ref, grad_in, grad_out,
    parts, gain, slots, sums, from_left, from_right, final, got, w_in, w_in_t, w_out, normed, cotangent, act, pre_grad,
    plane_send, plane_recv, ring_send, ring_recv, left_recv, right_recv, back_send, back_recv, weight_sem,
):
    here = place()
    column, half, core, zl = here
    me = column * 2 + core
    own = half * 4 + zl
    load_in = pltpu.make_async_copy(w_in_ref, w_in, weight_sem.at[0])
    load_out = pltpu.make_async_copy(w_out_ref, w_out, weight_sem.at[1])
    load_in.start()
    load_out.start()

    barrier = pltpu.get_barrier_semaphore()

    def signal(ahead, carry):
        _, target = plane_peer(*here, ahead)
        pl.semaphore_signal(barrier, inc=1, device_id=target, device_id_type=MESH)
        return carry

    lax.fori_loop(1, PEERS, signal, 0)
    for step in (-1, 1):
        pl.semaphore_signal(barrier, inc=1, device_id=z_neighbour(*here, step), device_id_type=MESH)

    for which, ref in enumerate((input_ref, cotangent_ref)):
        tokens = [ref[token].astype(jnp.float32).reshape(COLUMNS, 2, 2, 2, HEAD, 128) for token in range(2)]
        for to_half, to_core, head in ((a, b, c) for a in range(2) for b in range(2) for c in range(2)):
            both = jnp.stack([token[:, to_half, to_core, head] for token in tokens], axis=1)
            parts[to_half, head, :, to_core, which] = both.reshape(COLUMNS, 2 * HEAD, 128).astype(jnp.bfloat16)
    pl.semaphore_wait(barrier, PEERS + 1)

    phases = [(1 - half, OUT, 0), (1 - half, OUT, 1), (half, own, 0), (half, own, 1)]
    for which, (part, slot, head) in enumerate(phases):

        def send(ahead, carry, which=which, part=part, slot=slot, head=head):
            peer, target = plane_peer(*here, ahead)
            pltpu.make_async_remote_copy(
                src_ref=parts.at[part, head, peer // 2, lax.rem(peer, 2)],
                dst_ref=slots.at[slot, head, :, me],
                send_sem=plane_send.at[which],
                recv_sem=plane_recv.at[which],
                device_id=target,
                device_id_type=MESH,
            ).start()
            return carry

        lax.fori_loop(1, PEERS, send, 0)
        pltpu.make_async_copy(
            parts.at[part, head, column, core], slots.at[slot, head, :, me], plane_recv.at[which]
        ).start()

    def prepare():
        load_in.wait()
        load_out.wait()

        def turn(at, carry):
            token, chunk = at // 4, lax.rem(at, 4)
            rows = pl.ds(pl.multiple_of(chunk * 256, 256), 256)
            w_in_t[token, :, rows] = w_in[token, rows, :].T
            return carry

        lax.fori_loop(0, 8, turn, 0)
        for token in range(2):
            wide = jnp.broadcast_to(gain_ref[token : token + 1, :], (128, WIDTH)).T
            gain[token] = wide.reshape(COLUMNS, 2, 32, 128)

    targets = {"l": z_neighbour(*here, -1), "r": z_neighbour(*here, 1)}
    buffers = {"l": from_right, "r": from_left}
    arrivals = {"l": right_recv, "r": left_recv}

    def plane_of(name):
        k = int(name[1])
        return (1 - half) * 4 + k if name[0] == "c" else half * 4 + k

    def slot_of(name):
        return {"o": OUT, "p": PASS}.get(name) if name in "op" else plane_of(name)

    def end(case, head):
        total = sums[own, head].astype(jnp.float32)
        if case > 0:
            wait_for(from_left.at[own, head], left_recv.at[own, head])
            total = total + from_left[own, head].astype(jnp.float32)
        if case < 3:
            wait_for(from_right.at[own, head], right_recv.at[own, head])
            total = total + from_right[own, head].astype(jnp.float32)
        final[head, half] = total.astype(jnp.bfloat16)
        into, recv = (from_left, left_recv) if case < 2 else (from_right, right_recv)
        at = PLANES if case in (1, 2) else own
        wait_for(into.at[at, head], recv.at[at, head])
        final[head, 1 - half] = into[at, head]

        def send(ahead, carry):
            peer, target = plane_peer(*here, ahead)
            pltpu.make_async_remote_copy(
                src_ref=final.at[head, :, peer],
                dst_ref=got.at[head, me],
                send_sem=back_send.at[head],
                recv_sem=back_recv.at[head],
                device_id=target,
                device_id_type=MESH,
            ).start()
            return carry

        lax.fori_loop(1, PEERS, send, 0)
        pltpu.make_async_copy(final.at[head, :, me], got.at[head, me], back_recv.at[head]).start()

    def run(case, ops):
        for op in ops:
            if op[0] == "prepare":
                prepare()
                continue
            if op[0] == "end":
                end(case, op[1])
                continue
            if op[0] == "arrived":
                at, head = slot_of(op[1]), op[2]
                wait_for(slots.at[at, head], ring_recv.at[at, head])
                continue
            if op[0] in ("out", "own"):
                at, head = slot_of(op[1]), op[2]
                wait_for(slots.at[at, head], plane_recv.at[head + 2 * (op[0] == "own")])
                continue
            if op[0] == "sent":
                ref = slots.at[0, 0] if op[1] == "f" else sums.at[0, 0]
                wait_for(ref, ring_send.at["lr".index(op[2]), op[3]])
                continue
            way, name, head, turn = op[1], op[2], op[-2], op[-1]
            if op[0] == "f":
                at = slot_of(name)
                crosses = case == {"l": 0, "r": 3}[way]
                to = half * 4 + int(op[3][1]) if crosses else slot_of(op[3])
                from_ref, to_ref, recv = slots.at[at, head], slots.at[to, head], ring_recv.at[to, head]
            else:
                into, arrived = buffers[way], arrivals[way]
                at = to = plane_of(name)
                if name[0] == "p":
                    wait_for(into.at[at, head], arrived.at[at, head])
                    from_ref, to = into.at[at, head], PLANES
                elif case == {"l": 3, "r": 0}[way]:
                    from_ref = sums.at[at, head]
                else:
                    wait_for(into.at[at, head], arrived.at[at, head])
                    total = into[at, head].astype(jnp.float32) + sums[at, head].astype(jnp.float32)
                    into[at, head] = total.astype(jnp.bfloat16)
                    from_ref = into.at[at, head]
                to_ref, recv = into.at[to, head], arrived.at[to, head]
            pltpu.make_async_remote_copy(
                src_ref=from_ref,
                dst_ref=to_ref,
                send_sem=ring_send.at["lr".index(way), turn],
                recv_sem=recv,
                device_id=targets[way],
                device_id_type=MESH,
            ).start()

    plans = {case: steps_of(case) for case in range(4)}
    mlps = len(plans[0][1])

    def ahead_of(step, first, count):
        for case in range(4):

            @pl.when(zl == case)
            def _(case=case):
                for at in range(first, first + count):

                    @pl.when(step == at)
                    def _(at=at):
                        run(case, plans[case][0][at])

    def mlp(step, code):
        ahead_of(step, 0, mlps)
        k, head = lax.rem(code, 8) // 2, lax.rem(code, 2)
        columns = pl.ds(pl.multiple_of(k * 128, 128), 128)

        def mixed(zs):
            return slots[zs * 4 + k, head, 0].astype(jnp.float32).reshape(512, 128)

        squares = sum(jnp.sum(mixed(zs) ** 2, axis=0, keepdims=True) for zs in range(2))
        scale = lax.rsqrt(squares / WIDTH + EPS)
        for zs in range(2):
            value = (mixed(zs) * scale * gain[head, :, zs].reshape(512, 128)).astype(jnp.bfloat16)
            normed[head, :, zs, :, columns] = value.reshape(COLUMNS, 32, 128)
            cotangent[head, :, zs, :, columns] = slots[zs * 4 + k, head, 1].reshape(COLUMNS, 32, 128)
        plain = (((1,), (0,)))
        pre = dot(w_in_t[head], normed[head, :, :, :, columns].reshape(WIDTH, 128), plain)
        act_grad = dot(w_out[head], cotangent[head, :, :, :, columns].reshape(WIDTH, 128), plain)
        squared = pre * pre
        bend = jnp.tanh(0.7978845608 * (pre + 0.044715 * squared * pre))
        half_up = 0.5 * (1.0 + bend)
        act[head, :, columns] = (pre * half_up).astype(jnp.bfloat16)
        slope = half_up + 0.5 * pre * (1.0 - bend * bend) * (0.7978845608 * (1.0 + 0.134145 * squared))
        grad = (act_grad * slope).astype(jnp.bfloat16)
        pre_grad[head, :, columns] = grad
        upper = dot(w_in[head], grad, plain).reshape(COLUMNS, 2, 32, 128)
        upper = [upper[:, zs].reshape(512, 128) * gain[head, :, zs].reshape(512, 128) for zs in range(2)]
        inner = sum(jnp.sum(upper[zs] * mixed(zs), axis=0, keepdims=True) for zs in range(2))
        factor = scale * scale * scale * inner / WIDTH
        for zs in range(2):
            back = scale * upper[zs] - mixed(zs) * factor
            sums[zs * 4 + k, head] = back.astype(jnp.bfloat16).reshape(PEERS, 16, 128)
        return code // 8

    code = jnp.int32(0)
    for case in range(4):
        packed = sum((k * 2 + head) * 8**at for at, (k, head) in enumerate(plans[case][1]))
        code = jnp.where(zl == case, jnp.int32(packed), code)
    lax.fori_loop(0, mlps, mlp, code)

    def piece(step, carry):
        ahead_of(step + mlps, mlps, TAIL)
        head, part = step // 2, lax.rem(step, 2)
        turned = ((1,), (1,))
        rows = pl.ds(pl.multiple_of(part * 256, 256), 256)
        value = dot(act[head, rows, :], cotangent[head].reshape(WIDTH, 512), turned)
        grad_out[head, rows, :] = value.astype(jnp.bfloat16)
        groups = normed[head, pl.ds(part * 8, 8)].reshape(512, 512)
        rows = pl.ds(pl.multiple_of(part * 512, 512), 512)
        grad_in[head, rows, :] = dot(groups, pre_grad[head], turned).astype(jnp.bfloat16)
        return carry

    lax.fori_loop(0, TAIL, piece, 0)
    for case in range(4):

        @pl.when(zl == case)
        def _(case=case):
            run(case, plans[case][0][mlps + TAIL])

    for which in range(len(phases)):
        wait_for(got.at[0, pl.ds(0, PEERS - 1)], plane_send.at[which])
    for head in range(2):
        wait_for(got.at[head], back_recv.at[head])
    for from_half, from_core in ((a, b) for a in range(2) for b in range(2)):
        pair = []
        for head in range(2):
            rows = got[head, :, from_half].reshape(COLUMNS, 2, 2 * HEAD, 128)[:, from_core]
            pair.append(rows.astype(jnp.float32).reshape(COLUMNS, 2, HEAD, 128))
        for token in range(2):
            both = jnp.stack([rows[:, token] for rows in pair], axis=1).reshape(COLUMNS, 2 * HEAD, 128)
            returned_ref[token, :, from_half, from_core] = both.astype(jnp.bfloat16)
    for head in range(2):
        wait_for(got.at[head, pl.ds(0, PEERS - 1)], back_send.at[head])


def per_device(block_input, out_grad, norm_gain, w_in, w_out):
    own_rows, local_tok, width = block_input.shape
    rows = local_tok * HEAD
    hidden = w_in.shape[2]
    bf16 = jnp.bfloat16
    block = (PEERS, rows, own_rows)
    anywhere = pl.BlockSpec(memory_space=pl.ANY)
    inside = pl.BlockSpec(memory_space=pltpu.VMEM)
    dma = pltpu.SemaphoreType.DMA
    turned = out_grad.transpose(1, 2, 0)
    returned, grad_in, grad_out = pl.pallas_call(
        kernel,
        out_shape=(
            jax.ShapeDtypeStruct((local_tok, COLUMNS, 2, 2, rows, own_rows), bf16),
            jax.ShapeDtypeStruct(w_in.shape, bf16),
            jax.ShapeDtypeStruct(w_out.shape, bf16),
        ),
        in_specs=[inside, inside, inside, anywhere, anywhere],
        out_specs=(inside, inside, inside),
        scratch_shapes=[
            pltpu.VMEM((2, 2, COLUMNS, 2, 2, rows, own_rows), bf16),
            pltpu.VMEM((2, COLUMNS, 2, 2 * rows, own_rows), jnp.float32),
            pltpu.VMEM((PLANES + 2, 2, 2, *block), bf16),
            pltpu.VMEM((PLANES, 2, *block), bf16),
            pltpu.VMEM((PLANES + 1, 2, *block), bf16),
            pltpu.VMEM((PLANES + 1, 2, *block), bf16),
            pltpu.VMEM((2, 2, *block), bf16),
            pltpu.VMEM((2, PEERS, 2, rows, own_rows), bf16),
            pltpu.VMEM((2, width, hidden), bf16),
            pltpu.VMEM((2, hidden, width), bf16),
            pltpu.VMEM((2, hidden, width), bf16),
            pltpu.VMEM((2, COLUMNS, 2, 2 * rows, 4 * own_rows), bf16),
            pltpu.VMEM((2, COLUMNS, 2, 2 * rows, 4 * own_rows), bf16),
            pltpu.VMEM((2, hidden, 4 * own_rows), bf16),
            pltpu.VMEM((2, hidden, 4 * own_rows), bf16),
            dma((4,)),
            dma((4,)),
            dma((2, 24)),
            dma((PLANES + 2, 2)),
            dma((PLANES + 1, 2)),
            dma((PLANES + 1, 2)),
            dma((2,)),
            dma((2,)),
            dma((2,)),
        ],
        compiler_params=pltpu.CompilerParams(
            collective_id=0, has_side_effects=True, vmem_limit_bytes=46 * 2**20
        ),
    )(block_input.transpose(1, 2, 0), turned, norm_gain, w_in, w_out)
    returned = returned.reshape(local_tok, width, own_rows)
    input_grad = (turned.astype(jnp.float32) + returned.astype(jnp.float32)).astype(jnp.bfloat16)
    return (input_grad.transpose(2, 0, 1), grad_in, grad_out)


def solution(mesh):
    in_specs = (
        P("hid", "tok", None),
        P("hid", "tok", None),
        P("tok", None),
        P("tok", None, "hid"),
        P("tok", "hid", None),
    )
    out_specs = (P("hid", "tok", None), P("tok", None, "hid"), P("tok", "hid", None))
    return jax.shard_map(
        per_device, mesh=mesh, in_specs=in_specs, out_specs=out_specs, check_vma=False
    )
```

```python
import jax
import jax.numpy as jnp
from jax import lax
from jax.experimental import pallas as pl
from jax.experimental.pallas import tpu as pltpu
from jax.sharding import PartitionSpec as P

WIDTH = 1024
HEAD = 8
EPS = 1e-06
MESH = pl.DeviceIdType.MESH

COLUMNS = 16
PEERS = 32
PLANES = 8
OUT, PASS = 8, 9
DEPTH = 2
TAIL = 4

SEND, MLP, BACK, WEIGHTS, END = range(5)
NAMES = [f"{kind}{k}" for kind in "scp" for k in range(4)] + ["o", "p"]
ORDER = {
    0: [
        (0, 0, 12, 4, 0), (0, 0, 12, 4, 1), (0, 1, 7, 7, 0), (0, 0, 13, 5, 0), (0, 1, 7, 7, 1), (0, 0, 13, 5, 1),
        (0, 1, 6, 6, 0), (0, 1, 6, 6, 1), (0, 1, 0, 0, 0), (1, 2, 0), (2, 1, 2, 0), (0, 1, 0, 0, 1),
        (1, 0, 0), (2, 1, 4, 0), (1, 0, 1), (2, 1, 4, 1), (1, 1, 0), (2, 1, 5, 0),
        (2, 1, 1, 0), (1, 1, 1), (2, 1, 5, 1), (1, 2, 1), (2, 1, 2, 1), (2, 1, 1, 1),
        (1, 3, 0), (2, 1, 3, 0), (1, 3, 1), (2, 1, 3, 1), (2, 0, 6, 0), (2, 0, 6, 1),
        (2, 0, 7, 0), (2, 1, 9, 0), (2, 1, 9, 1), (2, 0, 7, 1), (4, 0), (3, 0),
        (4, 1), (3, 1), (3, 2), (3, 3),
    ],
    1: [
        (0, 0, 12, 13, 0), (0, 0, 12, 13, 1), (0, 1, 1, 1, 0), (0, 1, 1, 1, 1), (0, 0, 1, 1, 1), (0, 0, 2, 2, 0),
        (0, 1, 7, 7, 0), (0, 1, 7, 7, 1), (0, 0, 1, 1, 0), (0, 0, 4, 4, 0), (0, 1, 6, 6, 0), (1, 2, 0),
        (0, 0, 4, 4, 1), (0, 1, 6, 6, 1), (0, 0, 5, 5, 0), (1, 1, 0), (0, 0, 5, 5, 1), (2, 1, 2, 0),
        (0, 1, 0, 0, 0), (1, 1, 1), (1, 0, 1), (0, 1, 0, 0, 1), (0, 0, 2, 2, 1), (2, 1, 4, 1),
        (0, 0, 3, 3, 0), (2, 1, 5, 0), (0, 0, 3, 3, 1), (2, 1, 5, 1), (1, 3, 0), (1, 0, 0),
        (2, 1, 4, 0), (2, 0, 6, 0), (1, 2, 1), (2, 0, 6, 1), (2, 1, 2, 1), (2, 0, 7, 0),
        (2, 1, 3, 0), (1, 3, 1), (2, 0, 7, 1), (2, 1, 3, 1), (2, 0, 0, 0), (3, 0),
        (3, 1), (2, 0, 0, 1), (4, 0), (4, 1), (3, 2), (3, 3),
    ],
    2: [
        (0, 1, 12, 13, 0), (0, 1, 12, 13, 1), (0, 0, 2, 2, 0), (0, 0, 2, 2, 1), (0, 1, 2, 2, 1), (0, 1, 1, 1, 0),
        (0, 0, 4, 4, 0), (0, 0, 4, 4, 1), (0, 1, 2, 2, 0), (0, 1, 7, 7, 0), (0, 0, 5, 5, 0), (1, 1, 0),
        (0, 1, 7, 7, 1), (0, 0, 5, 5, 1), (0, 1, 6, 6, 0), (1, 2, 0), (0, 1, 6, 6, 1), (2, 0, 1, 0),
        (0, 0, 3, 3, 0), (1, 2, 1), (1, 3, 1), (0, 0, 3, 3, 1), (0, 1, 1, 1, 1), (2, 0, 7, 1),
        (0, 1, 0, 0, 0), (2, 0, 6, 0), (0, 1, 0, 0, 1), (2, 0, 6, 1), (1, 0, 0), (1, 3, 0),
        (2, 0, 7, 0), (2, 1, 5, 0), (1, 1, 1), (2, 1, 5, 1), (2, 0, 1, 1), (2, 1, 4, 0),
        (2, 0, 0, 0), (1, 0, 1), (2, 1, 4, 1), (2, 0, 0, 1), (2, 1, 3, 0), (3, 0),
        (3, 1), (2, 1, 3, 1), (4, 0), (4, 1), (3, 2), (3, 3),
    ],
    3: [
        (0, 1, 12, 7, 0), (0, 1, 12, 7, 1), (0, 0, 4, 4, 0), (0, 1, 13, 6, 0), (0, 0, 4, 4, 1), (0, 1, 13, 6, 1),
        (0, 0, 5, 5, 0), (0, 0, 5, 5, 1), (0, 0, 3, 3, 0), (1, 1, 0), (2, 0, 1, 0), (0, 0, 3, 3, 1),
        (1, 3, 0), (2, 0, 7, 0), (1, 3, 1), (2, 0, 7, 1), (1, 2, 0), (2, 0, 6, 0),
        (2, 0, 2, 0), (1, 2, 1), (2, 0, 6, 1), (1, 1, 1), (2, 0, 1, 1), (2, 0, 2, 1),
        (1, 0, 0), (2, 0, 0, 0), (1, 0, 1), (2, 0, 0, 1), (2, 1, 5, 0), (2, 1, 5, 1),
        (2, 1, 4, 0), (2, 0, 10, 0), (2, 0, 10, 1), (2, 1, 4, 1), (4, 0), (3, 0),
        (4, 1), (3, 1), (3, 2), (3, 3),
    ],
}


def place():
    tok, zl = lax.axis_index("tok"), lax.axis_index("hid")
    core, half, column = lax.rem(tok, 2), lax.rem(tok // 2, 2), tok // 4
    return column, half, core, zl


def device(column, half, core, zl):
    return (column * 4 + half * 2 + core, zl)


def z_neighbour(column, half, core, zl, step):
    z = lax.rem(half * 4 + zl + PLANES + step, PLANES)
    return device(column, z // 4, core, lax.rem(z, 4))


def plane_peer(column, half, core, zl, ahead):
    peer = lax.rem(column * 2 + core + ahead, PEERS)
    return peer, device(peer // 2, half, lax.rem(peer, 2), zl)


def wait_for(ref, sem):
    pltpu.make_async_copy(ref, ref, sem).wait()


def dot(left, right, dims):
    return lax.dot_general(left, right, (dims, ((), ())), preferred_element_type=jnp.float32)


def steps_of(case):
    parts, mlps, now = [], [], []
    here = set()
    sent = {"l": [], "r": []}

    def arrive(name, head):
        if (name, head) not in here:
            here.add((name, head))
            kind = {"o": "out", f"s{case}": "own"}.get(name, "arrived")
            now.append((kind, name, head))

    for kind, *item in ORDER[case]:
        if kind in (MLP, WEIGHTS):
            if kind == MLP:
                mlps.append(tuple(item))
                arrive(f"s{item[0]}", item[1])
                arrive(f"c{item[0]}", item[1])
            parts.append(now)
            now = []
            continue
        if kind == END:
            now.append(("end", item[0]))
            continue
        way, head = "lr"[item[0]], item[-1]
        names = [NAMES[at] for at in item[1:-1]]
        if kind == SEND:
            arrive(names[0], head)
        turns = sent[way]
        late = len(turns) - DEPTH
        if late >= 0:
            now.append(("sent", turns[late], way, late))
        turns.append("f" if kind == SEND else "b")
        now.append((turns[-1], way, *names, head, len(turns) - 1))
        if len(sent["l"]) + len(sent["r"]) == 3:
            now.append(("prepare",))
    parts.append(now)
    for way, turns in sent.items():
        parts[-1] += [("sent", turns[late], way, late) for late in range(max(0, len(turns) - DEPTH), len(turns))]
    return parts, mlps


def kernel(
    input_ref, cotangent_ref, gains_ref, w_in_ref, w_out_ref, returned_ref, grad_in, grad_out,
    parts, gains, gain, slots, sums, from_left, from_right, final, got, w_in, w_in_t, w_out, normed, cotangent, act, pre_grad,
    plane_send, plane_recv, ring_send, ring_recv, left_recv, right_recv, back_send, back_recv, weight_sem,
):
    here = place()
    column, half, core, zl = here
    me = column * 2 + core
    own = half * 4 + zl
    load_in = pltpu.make_async_copy(w_in_ref, w_in, weight_sem.at[0])
    load_out = pltpu.make_async_copy(w_out_ref, w_out, weight_sem.at[1])
    load_gain = pltpu.make_async_copy(gains_ref, gains, weight_sem.at[2])
    load_in.start()
    load_out.start()
    load_gain.start()

    barrier = pltpu.get_barrier_semaphore()

    def signal(ahead, carry):
        _, target = plane_peer(*here, ahead)
        pl.semaphore_signal(barrier, inc=1, device_id=target, device_id_type=MESH)
        return carry

    lax.fori_loop(1, PEERS, signal, 0)
    for step in (-1, 1):
        pl.semaphore_signal(barrier, inc=1, device_id=z_neighbour(*here, step), device_id_type=MESH)

    for which, ref in enumerate((input_ref, cotangent_ref)):
        tokens = [ref[token].astype(jnp.float32).reshape(COLUMNS, 2, 2, 2, HEAD, 128) for token in range(2)]
        for to_half, to_core, head in ((a, b, c) for a in range(2) for b in range(2) for c in range(2)):
            both = jnp.stack([token[:, to_half, to_core, head] for token in tokens], axis=1)
            parts[to_half, head, :, to_core, which] = both.reshape(COLUMNS, 2 * HEAD, 128).astype(jnp.bfloat16)
    pl.semaphore_wait(barrier, PEERS + 1)

    phases = [(1 - half, OUT, 0), (1 - half, OUT, 1), (half, own, 0), (half, own, 1)]
    for which, (part, slot, head) in enumerate(phases):

        def send(ahead, carry, which=which, part=part, slot=slot, head=head):
            peer, target = plane_peer(*here, ahead)
            pltpu.make_async_remote_copy(
                src_ref=parts.at[part, head, peer // 2, lax.rem(peer, 2)],
                dst_ref=slots.at[slot, head, :, me],
                send_sem=plane_send.at[which],
                recv_sem=plane_recv.at[which],
                device_id=target,
                device_id_type=MESH,
            ).start()
            return carry

        lax.fori_loop(1, PEERS, send, 0)
        pltpu.make_async_copy(
            parts.at[part, head, column, core], slots.at[slot, head, :, me], plane_recv.at[which]
        ).start()

    def prepare():
        load_in.wait()
        load_out.wait()
        load_gain.wait()

        def turn(at, carry):
            token, chunk = at // 4, lax.rem(at, 4)
            rows = pl.ds(pl.multiple_of(chunk * 256, 256), 256)
            w_in_t[token, :, rows] = w_in[token, rows, :].T
            return carry

        lax.fori_loop(0, 8, turn, 0)
        for token in range(2):
            wide = jnp.broadcast_to(gains[token : token + 1, :], (128, WIDTH)).T
            gain[token] = wide.reshape(COLUMNS, 2, 32, 128)

    targets = {"l": z_neighbour(*here, -1), "r": z_neighbour(*here, 1)}
    buffers = {"l": from_right, "r": from_left}
    arrivals = {"l": right_recv, "r": left_recv}

    def plane_of(name):
        k = int(name[1])
        return (1 - half) * 4 + k if name[0] == "c" else half * 4 + k

    def slot_of(name):
        return {"o": OUT, "p": PASS}.get(name) if name in "op" else plane_of(name)

    def end(case, head):
        total = sums[own, head].astype(jnp.float32)
        if case > 0:
            wait_for(from_left.at[own, head], left_recv.at[own, head])
            total = total + from_left[own, head].astype(jnp.float32)
        if case < 3:
            wait_for(from_right.at[own, head], right_recv.at[own, head])
            total = total + from_right[own, head].astype(jnp.float32)
        final[head, half] = total.astype(jnp.bfloat16)
        into, recv = (from_left, left_recv) if case < 2 else (from_right, right_recv)
        at = PLANES if case in (1, 2) else own
        wait_for(into.at[at, head], recv.at[at, head])
        final[head, 1 - half] = into[at, head]

        def send(ahead, carry):
            peer, target = plane_peer(*here, ahead)
            pltpu.make_async_remote_copy(
                src_ref=final.at[head, :, peer],
                dst_ref=got.at[head, me],
                send_sem=back_send.at[head],
                recv_sem=back_recv.at[head],
                device_id=target,
                device_id_type=MESH,
            ).start()
            return carry

        lax.fori_loop(1, PEERS, send, 0)
        pltpu.make_async_copy(final.at[head, :, me], got.at[head, me], back_recv.at[head]).start()

    def run(case, ops):
        for op in ops:
            if op[0] == "prepare":
                prepare()
                continue
            if op[0] == "end":
                end(case, op[1])
                continue
            if op[0] == "arrived":
                at, head = slot_of(op[1]), op[2]
                wait_for(slots.at[at, head], ring_recv.at[at, head])
                continue
            if op[0] in ("out", "own"):
                at, head = slot_of(op[1]), op[2]
                wait_for(slots.at[at, head], plane_recv.at[head + 2 * (op[0] == "own")])
                continue
            if op[0] == "sent":
                ref = slots.at[0, 0] if op[1] == "f" else sums.at[0, 0]
                wait_for(ref, ring_send.at["lr".index(op[2]), op[3]])
                continue
            way, name, head, turn = op[1], op[2], op[-2], op[-1]
            if op[0] == "f":
                at = slot_of(name)
                crosses = case == {"l": 0, "r": 3}[way]
                to = half * 4 + int(op[3][1]) if crosses else slot_of(op[3])
                from_ref, to_ref, recv = slots.at[at, head], slots.at[to, head], ring_recv.at[to, head]
            else:
                into, arrived = buffers[way], arrivals[way]
                at = to = plane_of(name)
                if name[0] == "p":
                    wait_for(into.at[at, head], arrived.at[at, head])
                    from_ref, to = into.at[at, head], PLANES
                elif case == {"l": 3, "r": 0}[way]:
                    from_ref = sums.at[at, head]
                else:
                    wait_for(into.at[at, head], arrived.at[at, head])
                    total = into[at, head].astype(jnp.float32) + sums[at, head].astype(jnp.float32)
                    into[at, head] = total.astype(jnp.bfloat16)
                    from_ref = into.at[at, head]
                to_ref, recv = into.at[to, head], arrived.at[to, head]
            pltpu.make_async_remote_copy(
                src_ref=from_ref,
                dst_ref=to_ref,
                send_sem=ring_send.at["lr".index(way), turn],
                recv_sem=recv,
                device_id=targets[way],
                device_id_type=MESH,
            ).start()

    plans = {case: steps_of(case) for case in range(4)}
    mlps = len(plans[0][1])

    def ahead_of(step, first, count):
        for case in range(4):

            @pl.when(zl == case)
            def _(case=case):
                for at in range(first, first + count):

                    @pl.when(step == at)
                    def _(at=at):
                        run(case, plans[case][0][at])

    def mlp(step, code):
        ahead_of(step, 0, mlps)
        k, head = lax.rem(code, 8) // 2, lax.rem(code, 2)
        columns = pl.ds(pl.multiple_of(k * 128, 128), 128)

        def mixed(zs):
            return slots[zs * 4 + k, head, 0].astype(jnp.float32).reshape(512, 128)

        squares = sum(jnp.sum(mixed(zs) ** 2, axis=0, keepdims=True) for zs in range(2))
        scale = lax.rsqrt(squares / WIDTH + EPS)
        for zs in range(2):
            value = (mixed(zs) * scale * gain[head, :, zs].reshape(512, 128)).astype(jnp.bfloat16)
            normed[head, :, zs, :, columns] = value.reshape(COLUMNS, 32, 128)
            cotangent[head, :, zs, :, columns] = slots[zs * 4 + k, head, 1].reshape(COLUMNS, 32, 128)
        plain = (((1,), (0,)))
        pre = dot(w_in_t[head], normed[head, :, :, :, columns].reshape(WIDTH, 128), plain)
        act_grad = dot(w_out[head], cotangent[head, :, :, :, columns].reshape(WIDTH, 128), plain)
        squared = pre * pre
        bend = jnp.tanh(0.7978845608 * (pre + 0.044715 * squared * pre))
        half_up = 0.5 * (1.0 + bend)
        act[head, :, columns] = (pre * half_up).astype(jnp.bfloat16)
        slope = half_up + 0.5 * pre * (1.0 - bend * bend) * (0.7978845608 * (1.0 + 0.134145 * squared))
        grad = (act_grad * slope).astype(jnp.bfloat16)
        pre_grad[head, :, columns] = grad
        upper = dot(w_in[head], grad, plain).reshape(COLUMNS, 2, 32, 128)
        upper = [upper[:, zs].reshape(512, 128) * gain[head, :, zs].reshape(512, 128) for zs in range(2)]
        inner = sum(jnp.sum(upper[zs] * mixed(zs), axis=0, keepdims=True) for zs in range(2))
        factor = scale * scale * scale * inner / WIDTH
        for zs in range(2):
            back = scale * upper[zs] - mixed(zs) * factor
            sums[zs * 4 + k, head] = back.astype(jnp.bfloat16).reshape(PEERS, 16, 128)
        return code // 8

    code = jnp.int32(0)
    for case in range(4):
        packed = sum((k * 2 + head) * 8**at for at, (k, head) in enumerate(plans[case][1]))
        code = jnp.where(zl == case, jnp.int32(packed), code)
    lax.fori_loop(0, mlps, mlp, code)

    def piece(step, carry):
        ahead_of(step + mlps, mlps, TAIL)
        head, part = step // 2, lax.rem(step, 2)
        turned = ((1,), (1,))
        rows = pl.ds(pl.multiple_of(part * 256, 256), 256)
        value = dot(act[head, rows, :], cotangent[head].reshape(WIDTH, 512), turned)
        grad_out[head, rows, :] = value.astype(jnp.bfloat16)
        groups = normed[head, pl.ds(part * 8, 8)].reshape(512, 512)
        rows = pl.ds(pl.multiple_of(part * 512, 512), 512)
        grad_in[head, rows, :] = dot(groups, pre_grad[head], turned).astype(jnp.bfloat16)
        return carry

    lax.fori_loop(0, TAIL, piece, 0)
    for case in range(4):

        @pl.when(zl == case)
        def _(case=case):
            run(case, plans[case][0][mlps + TAIL])

    for which in range(len(phases)):
        wait_for(got.at[0, pl.ds(0, PEERS - 1)], plane_send.at[which])
    for head in range(2):
        wait_for(got.at[head], back_recv.at[head])
    for from_half, from_core in ((a, b) for a in range(2) for b in range(2)):
        pair = []
        for head in range(2):
            rows = got[head, :, from_half].reshape(COLUMNS, 2, 2 * HEAD, 128)[:, from_core]
            pair.append(rows.astype(jnp.float32).reshape(COLUMNS, 2, HEAD, 128))
        for token in range(2):
            both = jnp.stack([rows[:, token] for rows in pair], axis=1).reshape(COLUMNS, 2 * HEAD, 128)
            returned_ref[token, :, from_half, from_core] = both.astype(jnp.bfloat16)
    for head in range(2):
        wait_for(got.at[head, pl.ds(0, PEERS - 1)], back_send.at[head])


def store(returned, turned, grad_in, grad_out, total, grad_in_out, grad_out_out, sems):
    copies = []
    for which, (ref, to) in enumerate(((grad_in, grad_in_out), (grad_out, grad_out_out))):
        for token in range(2):
            copies.append(pltpu.make_async_copy(ref.at[token], to.at[token], sems.at[which, token]))
    for copy in copies:
        copy.start()
    total[...] = (returned[...].astype(jnp.float32) + turned[...].astype(jnp.float32)).astype(jnp.bfloat16)
    for copy in copies:
        copy.wait()


def per_device(block_input, out_grad, norm_gain, w_in, w_out):
    own_rows, local_tok, width = block_input.shape
    rows = local_tok * HEAD
    hidden = w_in.shape[2]
    bf16 = jnp.bfloat16
    block = (PEERS, rows, own_rows)
    anywhere = pl.BlockSpec(memory_space=pl.ANY)
    inside = pl.BlockSpec(memory_space=pltpu.VMEM)
    dma = pltpu.SemaphoreType.DMA
    turned = out_grad.transpose(1, 2, 0)
    returned, grad_in, grad_out = pl.pallas_call(
        kernel,
        out_shape=(
            jax.ShapeDtypeStruct((local_tok, COLUMNS, 2, 2, rows, own_rows), bf16),
            jax.ShapeDtypeStruct(w_in.shape, bf16),
            jax.ShapeDtypeStruct(w_out.shape, bf16),
        ),
        in_specs=[inside, inside, anywhere, anywhere, anywhere],
        out_specs=(inside, inside, inside),
        scratch_shapes=[
            pltpu.VMEM((2, 2, COLUMNS, 2, 2, rows, own_rows), bf16),
            pltpu.VMEM((2, width), jnp.float32),
            pltpu.VMEM((2, COLUMNS, 2, 2 * rows, own_rows), jnp.float32),
            pltpu.VMEM((PLANES + 2, 2, 2, *block), bf16),
            pltpu.VMEM((PLANES, 2, *block), bf16),
            pltpu.VMEM((PLANES + 1, 2, *block), bf16),
            pltpu.VMEM((PLANES + 1, 2, *block), bf16),
            pltpu.VMEM((2, 2, *block), bf16),
            pltpu.VMEM((2, PEERS, 2, rows, own_rows), bf16),
            pltpu.VMEM((2, width, hidden), bf16),
            pltpu.VMEM((2, hidden, width), bf16),
            pltpu.VMEM((2, hidden, width), bf16),
            pltpu.VMEM((2, COLUMNS, 2, 2 * rows, 4 * own_rows), bf16),
            pltpu.VMEM((2, COLUMNS, 2, 2 * rows, 4 * own_rows), bf16),
            pltpu.VMEM((2, hidden, 4 * own_rows), bf16),
            pltpu.VMEM((2, hidden, 4 * own_rows), bf16),
            dma((4,)),
            dma((4,)),
            dma((2, 24)),
            dma((PLANES + 2, 2)),
            dma((PLANES + 1, 2)),
            dma((PLANES + 1, 2)),
            dma((2,)),
            dma((2,)),
            dma((3,)),
        ],
        compiler_params=pltpu.CompilerParams(
            collective_id=0, has_side_effects=True, vmem_limit_bytes=47 * 2**20
        ),
    )(block_input.transpose(1, 2, 0), turned, norm_gain, w_in, w_out)
    total, grad_in, grad_out = pl.pallas_call(
        store,
        out_shape=(
            jax.ShapeDtypeStruct(turned.shape, bf16),
            jax.ShapeDtypeStruct(w_in.shape, bf16),
            jax.ShapeDtypeStruct(w_out.shape, bf16),
        ),
        in_specs=[inside, inside, inside, inside],
        out_specs=(inside, anywhere, anywhere),
        scratch_shapes=[dma((2, 2))],
        compiler_params=pltpu.CompilerParams(vmem_limit_bytes=2**23),
    )(returned.reshape(turned.shape), turned, grad_in, grad_out)
    return (total.transpose(2, 0, 1), grad_in, grad_out)


def solution(mesh):
    in_specs = (
        P("hid", "tok", None),
        P("hid", "tok", None),
        P("tok", None),
        P("tok", None, "hid"),
        P("tok", "hid", None),
    )
    out_specs = (P("hid", "tok", None), P("tok", None, "hid"), P("tok", "hid", None))
    return jax.shard_map(
        per_device, mesh=mesh, in_specs=in_specs, out_specs=out_specs, check_vma=False
    )
```

```python
import jax
import jax.numpy as jnp
from jax import lax
from jax.experimental import pallas as pl
from jax.experimental.pallas import tpu as pltpu
from jax.sharding import PartitionSpec as P

WIDTH = 1024
HEAD = 8
EPS = 1e-06
MESH = pl.DeviceIdType.MESH

COLUMNS = 16
PEERS = 32
PLANES = 8
OUT, PASS = 8, 9
DEPTH = 2
TAIL = 4

SEND, MLP, BACK, WEIGHTS, END = range(5)
NAMES = [f"{kind}{k}" for kind in "scp" for k in range(4)] + ["o", "p"]
ORDER = {
    0: [
        (0, 0, 12, 4, 0), (0, 0, 12, 4, 1), (0, 0, 13, 5, 0), (0, 1, 7, 7, 0), (0, 1, 7, 7, 1), (0, 0, 13, 5, 1),
        (0, 1, 6, 6, 0), (0, 1, 6, 6, 1), (1, 2, 0), (0, 1, 0, 0, 0), (0, 1, 0, 0, 1), (1, 0, 0),
        (2, 1, 4, 0), (1, 0, 1), (2, 1, 4, 1), (2, 1, 2, 0), (1, 1, 0), (2, 1, 5, 0),
        (2, 1, 1, 0), (1, 1, 1), (2, 1, 5, 1), (2, 1, 1, 1), (1, 3, 0), (2, 1, 3, 0),
        (1, 3, 1), (2, 1, 3, 1), (2, 0, 6, 0), (1, 2, 1), (2, 1, 2, 1), (2, 0, 6, 1),
        (3, 0), (2, 0, 7, 1), (2, 1, 9, 0), (2, 0, 7, 0), (2, 1, 9, 1), (4, 1),
        (4, 0), (3, 1), (3, 2), (3, 3),
    ],
    1: [
        (0, 0, 12, 13, 0), (0, 0, 12, 13, 1), (0, 1, 1, 1, 0), (0, 1, 1, 1, 1), (0, 0, 1, 1, 1), (0, 0, 2, 2, 0),
        (0, 1, 7, 7, 0), (0, 0, 1, 1, 0), (0, 1, 7, 7, 1), (0, 0, 4, 4, 0), (0, 1, 6, 6, 0), (1, 2, 0),
        (0, 0, 4, 4, 1), (0, 1, 6, 6, 1), (1, 2, 1), (0, 0, 5, 5, 0), (0, 1, 0, 0, 0), (1, 0, 0),
        (0, 0, 5, 5, 1), (0, 1, 0, 0, 1), (1, 1, 0), (0, 0, 3, 3, 0), (2, 1, 4, 0), (0, 0, 3, 3, 1),
        (2, 1, 2, 0), (1, 3, 1), (2, 1, 5, 0), (1, 0, 1), (2, 1, 4, 1), (0, 0, 2, 2, 1),
        (1, 1, 1), (2, 1, 5, 1), (2, 0, 6, 0), (2, 0, 6, 1), (2, 0, 7, 1), (2, 1, 3, 1),
        (1, 3, 0), (2, 0, 7, 0), (2, 1, 3, 0), (3, 0), (3, 1), (2, 0, 0, 1),
        (2, 0, 0, 0), (2, 1, 2, 1), (3, 2), (4, 0), (4, 1), (3, 3),
    ],
    2: [
        (0, 1, 12, 13, 0), (0, 1, 12, 13, 1), (0, 0, 2, 2, 0), (0, 0, 2, 2, 1), (0, 1, 2, 2, 1), (0, 1, 1, 1, 0),
        (0, 0, 4, 4, 0), (0, 1, 2, 2, 0), (0, 0, 4, 4, 1), (0, 1, 7, 7, 0), (0, 0, 5, 5, 0), (1, 1, 0),
        (0, 1, 7, 7, 1), (0, 0, 5, 5, 1), (1, 1, 1), (0, 1, 6, 6, 0), (0, 0, 3, 3, 0), (1, 3, 0),
        (0, 1, 6, 6, 1), (0, 0, 3, 3, 1), (1, 2, 0), (0, 1, 0, 0, 0), (2, 0, 7, 0), (0, 1, 0, 0, 1),
        (2, 0, 1, 0), (1, 0, 1), (2, 0, 6, 0), (1, 3, 1), (2, 0, 7, 1), (0, 1, 1, 1, 1),
        (1, 2, 1), (2, 0, 6, 1), (2, 1, 5, 0), (2, 1, 5, 1), (2, 1, 4, 1), (2, 0, 0, 1),
        (1, 0, 0), (2, 1, 4, 0), (2, 0, 0, 0), (3, 0), (3, 1), (2, 1, 3, 1),
        (2, 1, 3, 0), (2, 0, 1, 1), (3, 2), (4, 0), (4, 1), (3, 3),
    ],
    3: [
        (0, 1, 12, 7, 0), (0, 1, 12, 7, 1), (0, 1, 13, 6, 0), (0, 0, 4, 4, 0), (0, 0, 4, 4, 1), (0, 1, 13, 6, 1),
        (0, 0, 5, 5, 0), (0, 0, 5, 5, 1), (1, 1, 0), (0, 0, 3, 3, 0), (0, 0, 3, 3, 1), (1, 3, 0),
        (2, 0, 7, 0), (1, 3, 1), (2, 0, 7, 1), (2, 0, 1, 0), (1, 2, 0), (2, 0, 6, 0),
        (2, 0, 2, 0), (1, 2, 1), (2, 0, 6, 1), (2, 0, 2, 1), (1, 0, 0), (2, 0, 0, 0),
        (1, 0, 1), (2, 0, 0, 1), (2, 1, 5, 0), (1, 1, 1), (2, 0, 1, 1), (2, 1, 5, 1),
        (3, 0), (2, 1, 4, 1), (2, 0, 10, 0), (2, 1, 4, 0), (2, 0, 10, 1), (4, 1),
        (4, 0), (3, 1), (3, 2), (3, 3),
    ],
}


def place():
    tok, zl = lax.axis_index("tok"), lax.axis_index("hid")
    core, half, column = lax.rem(tok, 2), lax.rem(tok // 2, 2), tok // 4
    return column, half, core, zl


def device(column, half, core, zl):
    return (column * 4 + half * 2 + core, zl)


def z_neighbour(column, half, core, zl, step):
    z = lax.rem(half * 4 + zl + PLANES + step, PLANES)
    return device(column, z // 4, core, lax.rem(z, 4))


def plane_peer(column, half, core, zl, ahead):
    peer = lax.rem(column * 2 + core + ahead, PEERS)
    return peer, device(peer // 2, half, lax.rem(peer, 2), zl)


def wait_for(ref, sem):
    pltpu.make_async_copy(ref, ref, sem).wait()


def dot(left, right, dims):
    return lax.dot_general(left, right, (dims, ((), ())), preferred_element_type=jnp.float32)


def steps_of(case):
    parts, mlps, now = [], [], []
    here = set()
    sent = {"l": [], "r": []}

    def arrive(name, head):
        if (name, head) not in here:
            here.add((name, head))
            kind = {"o": "out", f"s{case}": "own"}.get(name, "arrived")
            now.append((kind, name, head))

    for kind, *item in ORDER[case]:
        if kind in (MLP, WEIGHTS):
            if kind == MLP:
                mlps.append(tuple(item))
                arrive(f"s{item[0]}", item[1])
                arrive(f"c{item[0]}", item[1])
            parts.append(now)
            now = []
            continue
        if kind == END:
            now.append(("end", item[0]))
            continue
        way, head = "lr"[item[0]], item[-1]
        names = [NAMES[at] for at in item[1:-1]]
        if kind == SEND:
            arrive(names[0], head)
        turns = sent[way]
        late = len(turns) - DEPTH
        if late >= 0:
            now.append(("sent", turns[late], way, late))
        turns.append("f" if kind == SEND else "b")
        now.append((turns[-1], way, *names, head, len(turns) - 1))
        if len(sent["l"]) + len(sent["r"]) == 3:
            now.append(("prepare",))
    parts.append(now)
    for way, turns in sent.items():
        parts[-1] += [("sent", turns[late], way, late) for late in range(max(0, len(turns) - DEPTH), len(turns))]
    return parts, mlps


def kernel(
    input_ref, cotangent_ref, gains_ref, w_in_ref, w_out_ref, returned_ref, grad_in, grad_out,
    parts, gains, gain, slots, sums, from_left, from_right, final, got, w_in, w_in_t, w_out, normed, cotangent, act, pre_grad,
    plane_send, plane_recv, ring_send, ring_recv, left_recv, right_recv, back_send, back_recv, weight_sem,
):
    here = place()
    column, half, core, zl = here
    me = column * 2 + core
    own = half * 4 + zl
    load_in = pltpu.make_async_copy(w_in_ref, w_in, weight_sem.at[0])
    load_out = pltpu.make_async_copy(w_out_ref, w_out, weight_sem.at[1])
    load_gain = pltpu.make_async_copy(gains_ref, gains, weight_sem.at[2])
    load_in.start()
    load_out.start()
    load_gain.start()

    barrier = pltpu.get_barrier_semaphore()

    def signal(ahead, carry):
        _, target = plane_peer(*here, ahead)
        pl.semaphore_signal(barrier, inc=1, device_id=target, device_id_type=MESH)
        return carry

    lax.fori_loop(1, PEERS, signal, 0)
    for step in (-1, 1):
        pl.semaphore_signal(barrier, inc=1, device_id=z_neighbour(*here, step), device_id_type=MESH)

    for which, ref in enumerate((input_ref, cotangent_ref)):
        whole = ref[...].astype(jnp.float32)
        tokens = [whole[:, token, :].T.reshape(COLUMNS, 2, 2, 2, HEAD, 128) for token in range(2)]
        for to_half, to_core, head in ((a, b, c) for a in range(2) for b in range(2) for c in range(2)):
            both = jnp.stack([token[:, to_half, to_core, head] for token in tokens], axis=1)
            parts[to_half, head, :, to_core, which] = both.reshape(COLUMNS, 2 * HEAD, 128).astype(jnp.bfloat16)
    pl.semaphore_wait(barrier, PEERS + 1)

    phases = [(1 - half, OUT, 0), (1 - half, OUT, 1), (half, own, 0), (half, own, 1)]
    for which, (part, slot, head) in enumerate(phases):

        def send(ahead, carry, which=which, part=part, slot=slot, head=head):
            peer, target = plane_peer(*here, ahead)
            pltpu.make_async_remote_copy(
                src_ref=parts.at[part, head, peer // 2, lax.rem(peer, 2)],
                dst_ref=slots.at[slot, head, :, me],
                send_sem=plane_send.at[which],
                recv_sem=plane_recv.at[which],
                device_id=target,
                device_id_type=MESH,
            ).start()
            return carry

        lax.fori_loop(1, PEERS, send, 0)
        pltpu.make_async_copy(
            parts.at[part, head, column, core], slots.at[slot, head, :, me], plane_recv.at[which]
        ).start()

    def prepare():
        load_in.wait()
        load_out.wait()
        load_gain.wait()

        def turn(at, carry):
            token, chunk = at // 4, lax.rem(at, 4)
            rows = pl.ds(pl.multiple_of(chunk * 256, 256), 256)
            w_in_t[token, :, rows] = w_in[token, rows, :].T
            return carry

        lax.fori_loop(0, 8, turn, 0)
        for token in range(2):
            wide = jnp.broadcast_to(gains[token : token + 1, :], (128, WIDTH)).T
            gain[token] = wide.reshape(COLUMNS, 2, 32, 128)

    targets = {"l": z_neighbour(*here, -1), "r": z_neighbour(*here, 1)}
    buffers = {"l": from_right, "r": from_left}
    arrivals = {"l": right_recv, "r": left_recv}

    def plane_of(name):
        k = int(name[1])
        return (1 - half) * 4 + k if name[0] == "c" else half * 4 + k

    def slot_of(name):
        return {"o": OUT, "p": PASS}.get(name) if name in "op" else plane_of(name)

    def end(case, head):
        total = sums[own, head].astype(jnp.float32)
        if case > 0:
            wait_for(from_left.at[own, head], left_recv.at[own, head])
            total = total + from_left[own, head].astype(jnp.float32)
        if case < 3:
            wait_for(from_right.at[own, head], right_recv.at[own, head])
            total = total + from_right[own, head].astype(jnp.float32)
        final[head, half] = total.astype(jnp.bfloat16)
        into, recv = (from_left, left_recv) if case < 2 else (from_right, right_recv)
        at = PLANES if case in (1, 2) else own
        wait_for(into.at[at, head], recv.at[at, head])
        final[head, 1 - half] = into[at, head]

        def send(ahead, carry):
            peer, target = plane_peer(*here, ahead)
            pltpu.make_async_remote_copy(
                src_ref=final.at[head, :, peer],
                dst_ref=got.at[head, me],
                send_sem=back_send.at[head],
                recv_sem=back_recv.at[head],
                device_id=target,
                device_id_type=MESH,
            ).start()
            return carry

        lax.fori_loop(1, PEERS, send, 0)
        pltpu.make_async_copy(final.at[head, :, me], got.at[head, me], back_recv.at[head]).start()

    def run(case, ops):
        for op in ops:
            if op[0] == "prepare":
                prepare()
                continue
            if op[0] == "end":
                end(case, op[1])
                continue
            if op[0] == "arrived":
                at, head = slot_of(op[1]), op[2]
                wait_for(slots.at[at, head], ring_recv.at[at, head])
                continue
            if op[0] in ("out", "own"):
                at, head = slot_of(op[1]), op[2]
                wait_for(slots.at[at, head], plane_recv.at[head + 2 * (op[0] == "own")])
                continue
            if op[0] == "sent":
                ref = slots.at[0, 0] if op[1] == "f" else sums.at[0, 0]
                wait_for(ref, ring_send.at["lr".index(op[2]), op[3]])
                continue
            way, name, head, turn = op[1], op[2], op[-2], op[-1]
            if op[0] == "f":
                at = slot_of(name)
                crosses = case == {"l": 0, "r": 3}[way]
                to = half * 4 + int(op[3][1]) if crosses else slot_of(op[3])
                from_ref, to_ref, recv = slots.at[at, head], slots.at[to, head], ring_recv.at[to, head]
            else:
                into, arrived = buffers[way], arrivals[way]
                at = to = plane_of(name)
                if name[0] == "p":
                    wait_for(into.at[at, head], arrived.at[at, head])
                    from_ref, to = into.at[at, head], PLANES
                elif case == {"l": 3, "r": 0}[way]:
                    from_ref = sums.at[at, head]
                else:
                    wait_for(into.at[at, head], arrived.at[at, head])
                    total = into[at, head].astype(jnp.float32) + sums[at, head].astype(jnp.float32)
                    into[at, head] = total.astype(jnp.bfloat16)
                    from_ref = into.at[at, head]
                to_ref, recv = into.at[to, head], arrived.at[to, head]
            pltpu.make_async_remote_copy(
                src_ref=from_ref,
                dst_ref=to_ref,
                send_sem=ring_send.at["lr".index(way), turn],
                recv_sem=recv,
                device_id=targets[way],
                device_id_type=MESH,
            ).start()

    plans = {case: steps_of(case) for case in range(4)}
    mlps = len(plans[0][1])

    def ahead_of(step, first, count):
        for case in range(4):

            @pl.when(zl == case)
            def _(case=case):
                for at in range(first, first + count):

                    @pl.when(step == at)
                    def _(at=at):
                        run(case, plans[case][0][at])

    def mlp(step, code):
        ahead_of(step, 0, mlps)
        k, head = lax.rem(code, 8) // 2, lax.rem(code, 2)
        columns = pl.ds(pl.multiple_of(k * 128, 128), 128)

        def mixed(zs):
            return slots[zs * 4 + k, head, 0].astype(jnp.float32).reshape(512, 128)

        squares = sum(jnp.sum(mixed(zs) ** 2, axis=0, keepdims=True) for zs in range(2))
        scale = lax.rsqrt(squares / WIDTH + EPS)
        for zs in range(2):
            value = (mixed(zs) * scale * gain[head, :, zs].reshape(512, 128)).astype(jnp.bfloat16)
            normed[head, :, zs, :, columns] = value.reshape(COLUMNS, 32, 128)
            cotangent[head, :, zs, :, columns] = slots[zs * 4 + k, head, 1].reshape(COLUMNS, 32, 128)
        plain = (((1,), (0,)))
        pre = dot(w_in_t[head], normed[head, :, :, :, columns].reshape(WIDTH, 128), plain)
        act_grad = dot(w_out[head], cotangent[head, :, :, :, columns].reshape(WIDTH, 128), plain)
        squared = pre * pre
        bend = jnp.tanh(0.7978845608 * (pre + 0.044715 * squared * pre))
        half_up = 0.5 * (1.0 + bend)
        act[head, :, columns] = (pre * half_up).astype(jnp.bfloat16)
        slope = half_up + 0.5 * pre * (1.0 - bend * bend) * (0.7978845608 * (1.0 + 0.134145 * squared))
        grad = (act_grad * slope).astype(jnp.bfloat16)
        pre_grad[head, :, columns] = grad
        upper = dot(w_in[head], grad, plain).reshape(COLUMNS, 2, 32, 128)
        upper = [upper[:, zs].reshape(512, 128) * gain[head, :, zs].reshape(512, 128) for zs in range(2)]
        inner = sum(jnp.sum(upper[zs] * mixed(zs), axis=0, keepdims=True) for zs in range(2))
        factor = scale * scale * scale * inner / WIDTH
        for zs in range(2):
            back = scale * upper[zs] - mixed(zs) * factor
            sums[zs * 4 + k, head] = back.astype(jnp.bfloat16).reshape(PEERS, 16, 128)
        return code // 8

    code = jnp.int32(0)
    for case in range(4):
        packed = sum((k * 2 + head) * 8**at for at, (k, head) in enumerate(plans[case][1]))
        code = jnp.where(zl == case, jnp.int32(packed), code)
    lax.fori_loop(0, mlps, mlp, code)

    def piece(step, carry):
        ahead_of(step + mlps, mlps, TAIL)
        head, part = step // 2, lax.rem(step, 2)
        turned = ((1,), (1,))
        rows = pl.ds(pl.multiple_of(part * 256, 256), 256)
        value = dot(act[head, rows, :], cotangent[head].reshape(WIDTH, 512), turned)
        grad_out[head, rows, :] = value.astype(jnp.bfloat16)
        groups = normed[head, pl.ds(part * 8, 8)].reshape(512, 512)
        rows = pl.ds(pl.multiple_of(part * 512, 512), 512)
        grad_in[head, rows, :] = dot(groups, pre_grad[head], turned).astype(jnp.bfloat16)
        return carry

    lax.fori_loop(0, TAIL, piece, 0)
    for case in range(4):

        @pl.when(zl == case)
        def _(case=case):
            run(case, plans[case][0][mlps + TAIL])

    for which in range(len(phases)):
        wait_for(got.at[0, pl.ds(0, PEERS - 1)], plane_send.at[which])
    for head in range(2):
        wait_for(got.at[head], back_recv.at[head])
    for from_half, from_core in ((a, b) for a in range(2) for b in range(2)):
        pair = []
        for head in range(2):
            rows = got[head, :, from_half].reshape(COLUMNS, 2, 2 * HEAD, 128)[:, from_core]
            pair.append(rows.astype(jnp.float32).reshape(COLUMNS, 2, HEAD, 128))
        for token in range(2):
            both = jnp.stack([rows[:, token] for rows in pair], axis=1).reshape(COLUMNS, 2 * HEAD, 128)
            returned_ref[token, :, from_half, from_core] = both.astype(jnp.bfloat16)
    for head in range(2):
        wait_for(got.at[head, pl.ds(0, PEERS - 1)], back_send.at[head])


def store(returned, out_grad, grad_in, grad_out, total, grad_in_out, grad_out_out, sems):
    copies = []
    for which, (ref, to) in enumerate(((grad_in, grad_in_out), (grad_out, grad_out_out))):
        for token in range(2):
            copies.append(pltpu.make_async_copy(ref.at[token], to.at[token], sems.at[which, token]))
    for copy in copies:
        copy.start()
    both = jnp.stack([returned[token].astype(jnp.float32).T for token in range(2)], axis=1)
    total[...] = (both + out_grad[...].astype(jnp.float32)).astype(jnp.bfloat16)
    for copy in copies:
        copy.wait()


def per_device(block_input, out_grad, norm_gain, w_in, w_out):
    own_rows, local_tok, width = block_input.shape
    rows = local_tok * HEAD
    hidden = w_in.shape[2]
    bf16 = jnp.bfloat16
    block = (PEERS, rows, own_rows)
    anywhere = pl.BlockSpec(memory_space=pl.ANY)
    inside = pl.BlockSpec(memory_space=pltpu.VMEM)
    dma = pltpu.SemaphoreType.DMA
    returned, grad_in, grad_out = pl.pallas_call(
        kernel,
        out_shape=(
            jax.ShapeDtypeStruct((local_tok, COLUMNS, 2, 2, rows, own_rows), bf16),
            jax.ShapeDtypeStruct(w_in.shape, bf16),
            jax.ShapeDtypeStruct(w_out.shape, bf16),
        ),
        in_specs=[inside, inside, anywhere, anywhere, anywhere],
        out_specs=(inside, inside, inside),
        scratch_shapes=[
            pltpu.VMEM((2, 2, COLUMNS, 2, 2, rows, own_rows), bf16),
            pltpu.VMEM((2, width), jnp.float32),
            pltpu.VMEM((2, COLUMNS, 2, 2 * rows, own_rows), jnp.float32),
            pltpu.VMEM((PLANES + 2, 2, 2, *block), bf16),
            pltpu.VMEM((PLANES, 2, *block), bf16),
            pltpu.VMEM((PLANES + 1, 2, *block), bf16),
            pltpu.VMEM((PLANES + 1, 2, *block), bf16),
            pltpu.VMEM((2, 2, *block), bf16),
            pltpu.VMEM((2, PEERS, 2, rows, own_rows), bf16),
            pltpu.VMEM((2, width, hidden), bf16),
            pltpu.VMEM((2, hidden, width), bf16),
            pltpu.VMEM((2, hidden, width), bf16),
            pltpu.VMEM((2, COLUMNS, 2, 2 * rows, 4 * own_rows), bf16),
            pltpu.VMEM((2, COLUMNS, 2, 2 * rows, 4 * own_rows), bf16),
            pltpu.VMEM((2, hidden, 4 * own_rows), bf16),
            pltpu.VMEM((2, hidden, 4 * own_rows), bf16),
            dma((4,)),
            dma((4,)),
            dma((2, 24)),
            dma((PLANES + 2, 2)),
            dma((PLANES + 1, 2)),
            dma((PLANES + 1, 2)),
            dma((2,)),
            dma((2,)),
            dma((3,)),
        ],
        compiler_params=pltpu.CompilerParams(
            collective_id=0, has_side_effects=True, vmem_limit_bytes=47 * 2**20
        ),
    )(block_input, out_grad, norm_gain, w_in, w_out)
    total, grad_in, grad_out = pl.pallas_call(
        store,
        out_shape=(
            jax.ShapeDtypeStruct(out_grad.shape, bf16),
            jax.ShapeDtypeStruct(w_in.shape, bf16),
            jax.ShapeDtypeStruct(w_out.shape, bf16),
        ),
        in_specs=[inside, inside, inside, inside],
        out_specs=(inside, anywhere, anywhere),
        scratch_shapes=[dma((2, 2))],
        compiler_params=pltpu.CompilerParams(vmem_limit_bytes=2**23),
    )(returned.reshape(local_tok, width, own_rows), out_grad, grad_in, grad_out)
    return (total, grad_in, grad_out)


def solution(mesh):
    in_specs = (
        P("hid", "tok", None),
        P("hid", "tok", None),
        P("tok", None),
        P("tok", None, "hid"),
        P("tok", "hid", None),
    )
    out_specs = (P("hid", "tok", None), P("tok", None, "hid"), P("tok", "hid", None))
    return jax.shard_map(
        per_device, mesh=mesh, in_specs=in_specs, out_specs=out_specs, check_vma=False
    )
```

```python
import jax
import jax.numpy as jnp
from jax import lax
from jax.experimental import pallas as pl
from jax.experimental.pallas import tpu as pltpu
from jax.sharding import PartitionSpec as P

WIDTH = 1024
HEAD = 8
EPS = 1e-06
MESH = pl.DeviceIdType.MESH

COLUMNS = 16
PEERS = 32
PLANES = 8
OUT, PASS = 8, 9
DEPTH = 2
EARLY = 1
TAIL = 4

SEND, MLP, BACK, WEIGHTS, END = range(5)
NAMES = [f"{kind}{k}" for kind in "scp" for k in range(4)] + ["o", "p"]
ORDER = {
    0: [
        (0, 0, 12, 4, 0), (0, 0, 12, 4, 1), (0, 0, 13, 5, 0), (0, 1, 7, 7, 0), (0, 1, 7, 7, 1), (0, 0, 13, 5, 1),
        (0, 1, 6, 6, 0), (0, 1, 6, 6, 1), (1, 2, 0), (0, 1, 0, 0, 0), (0, 1, 0, 0, 1), (1, 0, 0),
        (2, 1, 4, 0), (1, 0, 1), (2, 1, 4, 1), (2, 1, 2, 0), (1, 1, 0), (2, 1, 5, 0),
        (2, 1, 1, 0), (1, 1, 1), (2, 1, 5, 1), (2, 1, 1, 1), (1, 3, 0), (2, 1, 3, 0),
        (1, 3, 1), (2, 1, 3, 1), (2, 0, 6, 0), (1, 2, 1), (2, 1, 2, 1), (2, 0, 6, 1),
        (3, 0), (2, 0, 7, 1), (2, 1, 9, 0), (2, 0, 7, 0), (2, 1, 9, 1), (4, 1),
        (4, 0), (3, 1), (3, 2), (3, 3),
    ],
    1: [
        (0, 0, 12, 13, 0), (0, 0, 12, 13, 1), (0, 1, 1, 1, 0), (0, 1, 1, 1, 1), (0, 0, 1, 1, 1), (0, 0, 2, 2, 0),
        (0, 1, 7, 7, 0), (0, 0, 1, 1, 0), (0, 1, 7, 7, 1), (0, 0, 4, 4, 0), (0, 1, 6, 6, 0), (1, 2, 0),
        (0, 0, 4, 4, 1), (0, 1, 6, 6, 1), (1, 2, 1), (0, 0, 5, 5, 0), (0, 1, 0, 0, 0), (1, 0, 0),
        (0, 0, 5, 5, 1), (0, 1, 0, 0, 1), (1, 1, 0), (0, 0, 3, 3, 0), (2, 1, 4, 0), (0, 0, 3, 3, 1),
        (2, 1, 2, 0), (1, 3, 1), (2, 1, 5, 0), (1, 0, 1), (2, 1, 4, 1), (0, 0, 2, 2, 1),
        (1, 1, 1), (2, 1, 5, 1), (2, 0, 6, 0), (2, 0, 6, 1), (2, 0, 7, 1), (2, 1, 3, 1),
        (1, 3, 0), (2, 0, 7, 0), (2, 1, 3, 0), (3, 0), (3, 1), (2, 0, 0, 1),
        (2, 0, 0, 0), (2, 1, 2, 1), (3, 2), (4, 0), (4, 1), (3, 3),
    ],
    2: [
        (0, 1, 12, 13, 0), (0, 1, 12, 13, 1), (0, 0, 2, 2, 0), (0, 0, 2, 2, 1), (0, 1, 2, 2, 1), (0, 1, 1, 1, 0),
        (0, 0, 4, 4, 0), (0, 1, 2, 2, 0), (0, 0, 4, 4, 1), (0, 1, 7, 7, 0), (0, 0, 5, 5, 0), (1, 1, 0),
        (0, 1, 7, 7, 1), (0, 0, 5, 5, 1), (1, 1, 1), (0, 1, 6, 6, 0), (0, 0, 3, 3, 0), (1, 3, 0),
        (0, 1, 6, 6, 1), (0, 0, 3, 3, 1), (1, 2, 0), (0, 1, 0, 0, 0), (2, 0, 7, 0), (0, 1, 0, 0, 1),
        (2, 0, 1, 0), (1, 0, 1), (2, 0, 6, 0), (1, 3, 1), (2, 0, 7, 1), (0, 1, 1, 1, 1),
        (1, 2, 1), (2, 0, 6, 1), (2, 1, 5, 0), (2, 1, 5, 1), (2, 1, 4, 1), (2, 0, 0, 1),
        (1, 0, 0), (2, 1, 4, 0), (2, 0, 0, 0), (3, 0), (3, 1), (2, 1, 3, 1),
        (2, 1, 3, 0), (2, 0, 1, 1), (3, 2), (4, 0), (4, 1), (3, 3),
    ],
    3: [
        (0, 1, 12, 7, 0), (0, 1, 12, 7, 1), (0, 1, 13, 6, 0), (0, 0, 4, 4, 0), (0, 0, 4, 4, 1), (0, 1, 13, 6, 1),
        (0, 0, 5, 5, 0), (0, 0, 5, 5, 1), (1, 1, 0), (0, 0, 3, 3, 0), (0, 0, 3, 3, 1), (1, 3, 0),
        (2, 0, 7, 0), (1, 3, 1), (2, 0, 7, 1), (2, 0, 1, 0), (1, 2, 0), (2, 0, 6, 0),
        (2, 0, 2, 0), (1, 2, 1), (2, 0, 6, 1), (2, 0, 2, 1), (1, 0, 0), (2, 0, 0, 0),
        (1, 0, 1), (2, 0, 0, 1), (2, 1, 5, 0), (1, 1, 1), (2, 0, 1, 1), (2, 1, 5, 1),
        (3, 0), (2, 1, 4, 1), (2, 0, 10, 0), (2, 1, 4, 0), (2, 0, 10, 1), (4, 1),
        (4, 0), (3, 1), (3, 2), (3, 3),
    ],
}


def place():
    tok, zl = lax.axis_index("tok"), lax.axis_index("hid")
    core, half, column = lax.rem(tok, 2), lax.rem(tok // 2, 2), tok // 4
    return column, half, core, zl


def device(column, half, core, zl):
    return (column * 4 + half * 2 + core, zl)


def z_neighbour(column, half, core, zl, step):
    z = lax.rem(half * 4 + zl + PLANES + step, PLANES)
    return device(column, z // 4, core, lax.rem(z, 4))


def plane_peer(column, half, core, zl, ahead):
    peer = lax.rem(column * 2 + core + ahead, PEERS)
    return peer, device(peer // 2, half, lax.rem(peer, 2), zl)


def wait_for(ref, sem):
    pltpu.make_async_copy(ref, ref, sem).wait()


def dot(left, right, dims):
    return lax.dot_general(left, right, (dims, ((), ())), preferred_element_type=jnp.float32)


def steps_of(case):
    parts, mlps, now = [], [], []
    here = set()
    sent = {"l": [], "r": []}

    def arrive(name, head):
        if (name, head) not in here:
            here.add((name, head))
            kind = {"o": "out", f"s{case}": "own"}.get(name, "arrived")
            now.append((kind, name, head))

    for kind, *item in ORDER[case]:
        if kind in (MLP, WEIGHTS):
            if kind == MLP:
                mlps.append(tuple(item))
                arrive(f"s{item[0]}", item[1])
                arrive(f"c{item[0]}", item[1])
            parts.append(now)
            now = []
            continue
        if kind == END:
            now.append(("end", item[0]))
            continue
        way, head = "lr"[item[0]], item[-1]
        names = [NAMES[at] for at in item[1:-1]]
        if kind == SEND:
            arrive(names[0], head)
        turns = sent[way]
        late = len(turns) - DEPTH
        if late >= 0:
            now.append(("sent", turns[late], way, late))
        turns.append("f" if kind == SEND else "b")
        now.append((turns[-1], way, *names, head, len(turns) - 1))
        if len(sent["l"]) + len(sent["r"]) == 1:
            now += [("exchange", which) for which in range(EARLY, 4)]
        if len(sent["l"]) + len(sent["r"]) == 3:
            now.append(("prepare",))
    parts.append(now)
    for way, turns in sent.items():
        parts[-1] += [("sent", turns[late], way, late) for late in range(max(0, len(turns) - DEPTH), len(turns))]
    return parts, mlps


def kernel(
    input_ref, cotangent_ref, gains_ref, w_in_ref, w_out_ref, returned_ref, grad_in, grad_out,
    parts, gains, gain, slots, sums, from_left, from_right, final, got, w_in, w_in_t, w_out, normed, cotangent, act, pre_grad,
    plane_send, plane_recv, ring_send, ring_recv, left_recv, right_recv, back_send, back_recv, weight_sem,
):
    here = place()
    column, half, core, zl = here
    me = column * 2 + core
    own = half * 4 + zl
    load_in = pltpu.make_async_copy(w_in_ref, w_in, weight_sem.at[0])
    load_out = pltpu.make_async_copy(w_out_ref, w_out, weight_sem.at[1])
    load_gain = pltpu.make_async_copy(gains_ref, gains, weight_sem.at[2])
    load_in.start()
    load_out.start()
    load_gain.start()

    barrier = pltpu.get_barrier_semaphore()

    def signal(ahead, carry):
        _, target = plane_peer(*here, ahead)
        pl.semaphore_signal(barrier, inc=1, device_id=target, device_id_type=MESH)
        return carry

    lax.fori_loop(1, PEERS, signal, 0)
    for step in (-1, 1):
        pl.semaphore_signal(barrier, inc=1, device_id=z_neighbour(*here, step), device_id_type=MESH)

    for which, ref in enumerate((input_ref, cotangent_ref)):
        whole = ref[...].astype(jnp.float32)
        tokens = [whole[:, token, :].T.reshape(COLUMNS, 2, 2, 2, HEAD, 128) for token in range(2)]
        for to_half, to_core, head in ((a, b, c) for a in range(2) for b in range(2) for c in range(2)):
            both = jnp.stack([token[:, to_half, to_core, head] for token in tokens], axis=1)
            parts[to_half, head, :, to_core, which] = both.reshape(COLUMNS, 2 * HEAD, 128).astype(jnp.bfloat16)
    pl.semaphore_wait(barrier, PEERS + 1)

    phases = [(1 - half, OUT, 0), (1 - half, OUT, 1), (half, own, 0), (half, own, 1)]

    def exchange(which):
        part, slot, head = phases[which]

        def send(ahead, carry):
            peer, target = plane_peer(*here, ahead)
            pltpu.make_async_remote_copy(
                src_ref=parts.at[part, head, peer // 2, lax.rem(peer, 2)],
                dst_ref=slots.at[slot, head, :, me],
                send_sem=plane_send.at[which],
                recv_sem=plane_recv.at[which],
                device_id=target,
                device_id_type=MESH,
            ).start()
            return carry

        lax.fori_loop(1, PEERS, send, 0)
        pltpu.make_async_copy(
            parts.at[part, head, column, core], slots.at[slot, head, :, me], plane_recv.at[which]
        ).start()

    for which in range(EARLY):
        exchange(which)

    def prepare():
        load_in.wait()
        load_out.wait()
        load_gain.wait()

        def turn(at, carry):
            token, chunk = at // 4, lax.rem(at, 4)
            rows = pl.ds(pl.multiple_of(chunk * 256, 256), 256)
            w_in_t[token, :, rows] = w_in[token, rows, :].T
            return carry

        lax.fori_loop(0, 8, turn, 0)
        for token in range(2):
            wide = jnp.broadcast_to(gains[token : token + 1, :], (128, WIDTH)).T
            gain[token] = wide.reshape(COLUMNS, 2, 32, 128)

    targets = {"l": z_neighbour(*here, -1), "r": z_neighbour(*here, 1)}
    buffers = {"l": from_right, "r": from_left}
    arrivals = {"l": right_recv, "r": left_recv}

    def plane_of(name):
        k = int(name[1])
        return (1 - half) * 4 + k if name[0] == "c" else half * 4 + k

    def slot_of(name):
        return {"o": OUT, "p": PASS}.get(name) if name in "op" else plane_of(name)

    def end(case, head):
        total = sums[own, head].astype(jnp.float32)
        if case > 0:
            wait_for(from_left.at[own, head], left_recv.at[own, head])
            total = total + from_left[own, head].astype(jnp.float32)
        if case < 3:
            wait_for(from_right.at[own, head], right_recv.at[own, head])
            total = total + from_right[own, head].astype(jnp.float32)
        final[head, half] = total.astype(jnp.bfloat16)
        into, recv = (from_left, left_recv) if case < 2 else (from_right, right_recv)
        at = PLANES if case in (1, 2) else own
        wait_for(into.at[at, head], recv.at[at, head])
        final[head, 1 - half] = into[at, head]

        def send(ahead, carry):
            peer, target = plane_peer(*here, ahead)
            pltpu.make_async_remote_copy(
                src_ref=final.at[head, :, peer],
                dst_ref=got.at[head, me],
                send_sem=back_send.at[head],
                recv_sem=back_recv.at[head],
                device_id=target,
                device_id_type=MESH,
            ).start()
            return carry

        lax.fori_loop(1, PEERS, send, 0)
        pltpu.make_async_copy(final.at[head, :, me], got.at[head, me], back_recv.at[head]).start()

    def run(case, ops):
        for op in ops:
            if op[0] == "exchange":
                exchange(op[1])
                continue
            if op[0] == "prepare":
                prepare()
                continue
            if op[0] == "end":
                end(case, op[1])
                continue
            if op[0] == "arrived":
                at, head = slot_of(op[1]), op[2]
                wait_for(slots.at[at, head], ring_recv.at[at, head])
                continue
            if op[0] in ("out", "own"):
                at, head = slot_of(op[1]), op[2]
                wait_for(slots.at[at, head], plane_recv.at[head + 2 * (op[0] == "own")])
                continue
            if op[0] == "sent":
                ref = slots.at[0, 0] if op[1] == "f" else sums.at[0, 0]
                wait_for(ref, ring_send.at["lr".index(op[2]), op[3]])
                continue
            way, name, head, turn = op[1], op[2], op[-2], op[-1]
            if op[0] == "f":
                at = slot_of(name)
                crosses = case == {"l": 0, "r": 3}[way]
                to = half * 4 + int(op[3][1]) if crosses else slot_of(op[3])
                from_ref, to_ref, recv = slots.at[at, head], slots.at[to, head], ring_recv.at[to, head]
            else:
                into, arrived = buffers[way], arrivals[way]
                at = to = plane_of(name)
                if name[0] == "p":
                    wait_for(into.at[at, head], arrived.at[at, head])
                    from_ref, to = into.at[at, head], PLANES
                elif case == {"l": 3, "r": 0}[way]:
                    from_ref = sums.at[at, head]
                else:
                    wait_for(into.at[at, head], arrived.at[at, head])
                    total = into[at, head].astype(jnp.float32) + sums[at, head].astype(jnp.float32)
                    into[at, head] = total.astype(jnp.bfloat16)
                    from_ref = into.at[at, head]
                to_ref, recv = into.at[to, head], arrived.at[to, head]
            pltpu.make_async_remote_copy(
                src_ref=from_ref,
                dst_ref=to_ref,
                send_sem=ring_send.at["lr".index(way), turn],
                recv_sem=recv,
                device_id=targets[way],
                device_id_type=MESH,
            ).start()

    plans = {case: steps_of(case) for case in range(4)}
    mlps = len(plans[0][1])

    def ahead_of(step, first, count):
        for case in range(4):

            @pl.when(zl == case)
            def _(case=case):
                for at in range(first, first + count):

                    @pl.when(step == at)
                    def _(at=at):
                        run(case, plans[case][0][at])

    def mlp(step, code):
        ahead_of(step, 0, mlps)
        k, head = lax.rem(code, 8) // 2, lax.rem(code, 2)
        columns = pl.ds(pl.multiple_of(k * 128, 128), 128)

        def mixed(zs):
            return slots[zs * 4 + k, head, 0].astype(jnp.float32).reshape(512, 128)

        squares = sum(jnp.sum(mixed(zs) ** 2, axis=0, keepdims=True) for zs in range(2))
        scale = lax.rsqrt(squares / WIDTH + EPS)
        for zs in range(2):
            value = (mixed(zs) * scale * gain[head, :, zs].reshape(512, 128)).astype(jnp.bfloat16)
            normed[head, :, zs, :, columns] = value.reshape(COLUMNS, 32, 128)
            cotangent[head, :, zs, :, columns] = slots[zs * 4 + k, head, 1].reshape(COLUMNS, 32, 128)
        plain = (((1,), (0,)))
        pre = dot(w_in_t[head], normed[head, :, :, :, columns].reshape(WIDTH, 128), plain)
        act_grad = dot(w_out[head], cotangent[head, :, :, :, columns].reshape(WIDTH, 128), plain)
        squared = pre * pre
        bend = jnp.tanh(0.7978845608 * (pre + 0.044715 * squared * pre))
        half_up = 0.5 * (1.0 + bend)
        act[head, :, columns] = (pre * half_up).astype(jnp.bfloat16)
        slope = half_up + 0.5 * pre * (1.0 - bend * bend) * (0.7978845608 * (1.0 + 0.134145 * squared))
        grad = (act_grad * slope).astype(jnp.bfloat16)
        pre_grad[head, :, columns] = grad
        upper = dot(w_in[head], grad, plain).reshape(COLUMNS, 2, 32, 128)
        upper = [upper[:, zs].reshape(512, 128) * gain[head, :, zs].reshape(512, 128) for zs in range(2)]
        inner = sum(jnp.sum(upper[zs] * mixed(zs), axis=0, keepdims=True) for zs in range(2))
        factor = scale * scale * scale * inner / WIDTH
        for zs in range(2):
            back = scale * upper[zs] - mixed(zs) * factor
            sums[zs * 4 + k, head] = back.astype(jnp.bfloat16).reshape(PEERS, 16, 128)
        return code // 8

    code = jnp.int32(0)
    for case in range(4):
        packed = sum((k * 2 + head) * 8**at for at, (k, head) in enumerate(plans[case][1]))
        code = jnp.where(zl == case, jnp.int32(packed), code)
    lax.fori_loop(0, mlps, mlp, code)

    def piece(step, carry):
        ahead_of(step + mlps, mlps, TAIL)
        head, part = step // 2, lax.rem(step, 2)
        turned = ((1,), (1,))
        rows = pl.ds(pl.multiple_of(part * 256, 256), 256)
        value = dot(act[head, rows, :], cotangent[head].reshape(WIDTH, 512), turned)
        grad_out[head, rows, :] = value.astype(jnp.bfloat16)
        groups = normed[head, pl.ds(part * 8, 8)].reshape(512, 512)
        rows = pl.ds(pl.multiple_of(part * 512, 512), 512)
        grad_in[head, rows, :] = dot(groups, pre_grad[head], turned).astype(jnp.bfloat16)
        return carry

    lax.fori_loop(0, TAIL, piece, 0)
    for case in range(4):

        @pl.when(zl == case)
        def _(case=case):
            run(case, plans[case][0][mlps + TAIL])

    for which in range(len(phases)):
        wait_for(got.at[0, pl.ds(0, PEERS - 1)], plane_send.at[which])
    for head in range(2):
        wait_for(got.at[head], back_recv.at[head])
    for from_half, from_core in ((a, b) for a in range(2) for b in range(2)):
        pair = []
        for head in range(2):
            rows = got[head, :, from_half].reshape(COLUMNS, 2, 2 * HEAD, 128)[:, from_core]
            pair.append(rows.astype(jnp.float32).reshape(COLUMNS, 2, HEAD, 128))
        for token in range(2):
            both = jnp.stack([rows[:, token] for rows in pair], axis=1).reshape(COLUMNS, 2 * HEAD, 128)
            returned_ref[token, :, from_half, from_core] = both.astype(jnp.bfloat16)
    for head in range(2):
        wait_for(got.at[head, pl.ds(0, PEERS - 1)], back_send.at[head])


def store(returned, out_grad, grad_in, grad_out, total, grad_in_out, grad_out_out, sems):
    copies = []
    for which, (ref, to) in enumerate(((grad_in, grad_in_out), (grad_out, grad_out_out))):
        for token in range(2):
            copies.append(pltpu.make_async_copy(ref.at[token], to.at[token], sems.at[which, token]))
    for copy in copies:
        copy.start()
    for rows in range(0, WIDTH, 256):
        columns = slice(rows, rows + 256)
        both = jnp.stack([returned[token, columns].T.astype(jnp.float32) for token in range(2)], axis=1)
        total[:, :, columns] = (both + out_grad[:, :, columns].astype(jnp.float32)).astype(jnp.bfloat16)
    for copy in copies:
        copy.wait()


def per_device(block_input, out_grad, norm_gain, w_in, w_out):
    own_rows, local_tok, width = block_input.shape
    rows = local_tok * HEAD
    hidden = w_in.shape[2]
    bf16 = jnp.bfloat16
    block = (PEERS, rows, own_rows)
    anywhere = pl.BlockSpec(memory_space=pl.ANY)
    inside = pl.BlockSpec(memory_space=pltpu.VMEM)
    dma = pltpu.SemaphoreType.DMA
    returned, grad_in, grad_out = pl.pallas_call(
        kernel,
        out_shape=(
            jax.ShapeDtypeStruct((local_tok, COLUMNS, 2, 2, rows, own_rows), bf16),
            jax.ShapeDtypeStruct(w_in.shape, bf16),
            jax.ShapeDtypeStruct(w_out.shape, bf16),
        ),
        in_specs=[inside, inside, anywhere, anywhere, anywhere],
        out_specs=(inside, inside, inside),
        scratch_shapes=[
            pltpu.VMEM((2, 2, COLUMNS, 2, 2, rows, own_rows), bf16),
            pltpu.VMEM((2, width), jnp.float32),
            pltpu.VMEM((2, COLUMNS, 2, 2 * rows, own_rows), jnp.float32),
            pltpu.VMEM((PLANES + 2, 2, 2, *block), bf16),
            pltpu.VMEM((PLANES, 2, *block), bf16),
            pltpu.VMEM((PLANES + 1, 2, *block), bf16),
            pltpu.VMEM((PLANES + 1, 2, *block), bf16),
            pltpu.VMEM((2, 2, *block), bf16),
            pltpu.VMEM((2, PEERS, 2, rows, own_rows), bf16),
            pltpu.VMEM((2, width, hidden), bf16),
            pltpu.VMEM((2, hidden, width), bf16),
            pltpu.VMEM((2, hidden, width), bf16),
            pltpu.VMEM((2, COLUMNS, 2, 2 * rows, 4 * own_rows), bf16),
            pltpu.VMEM((2, COLUMNS, 2, 2 * rows, 4 * own_rows), bf16),
            pltpu.VMEM((2, hidden, 4 * own_rows), bf16),
            pltpu.VMEM((2, hidden, 4 * own_rows), bf16),
            dma((4,)),
            dma((4,)),
            dma((2, 24)),
            dma((PLANES + 2, 2)),
            dma((PLANES + 1, 2)),
            dma((PLANES + 1, 2)),
            dma((2,)),
            dma((2,)),
            dma((3,)),
        ],
        compiler_params=pltpu.CompilerParams(
            collective_id=0, has_side_effects=True, vmem_limit_bytes=47 * 2**20
        ),
    )(block_input, out_grad, norm_gain, w_in, w_out)
    total, grad_in, grad_out = pl.pallas_call(
        store,
        out_shape=(
            jax.ShapeDtypeStruct(out_grad.shape, bf16),
            jax.ShapeDtypeStruct(w_in.shape, bf16),
            jax.ShapeDtypeStruct(w_out.shape, bf16),
        ),
        in_specs=[inside, inside, inside, inside],
        out_specs=(inside, anywhere, anywhere),
        scratch_shapes=[dma((2, 2))],
        compiler_params=pltpu.CompilerParams(vmem_limit_bytes=2**23),
    )(returned.reshape(local_tok, width, own_rows), out_grad, grad_in, grad_out)
    return (total, grad_in, grad_out)


def solution(mesh):
    in_specs = (
        P("hid", "tok", None),
        P("hid", "tok", None),
        P("tok", None),
        P("tok", None, "hid"),
        P("tok", "hid", None),
    )
    out_specs = (P("hid", "tok", None), P("tok", None, "hid"), P("tok", "hid", None))
    return jax.shard_map(
        per_device, mesh=mesh, in_specs=in_specs, out_specs=out_specs, check_vma=False
    )
```
